128 devices in a mesh: dp: 8 (over z_lo, x), seq: 16 (over y, z_hi, core).
Axes of the slice: x: 4, y: 4, z: 4 (z_hi: 2, z_lo: 2; z = z_hi * 2 + z_lo), core: 2. Of those that a mesh axis runs over, the one named last changes fastest.
Arguments:
- item_table: float32 [4096, 512], P('dp'), may hold values from -40 to 40
- serve_lists: int32 [8, 8, 16, 128], P('dp', None, 'seq'), may hold values from 0 to 511, as said below
- event_slots: int32 [8, 2, 4096], P('dp', None, 'seq'), may hold values from 0 to 1023, as said below
- session_tiles: int32 [8, 32, 32], P('dp', 'seq'), may hold values from 0 to 1, as said below
- w_query: float32 [512, 512], replicated, may hold values from -1 to 1
- w_key: float32 [512, 512], replicated, may hold values from -1 to 1
- w_value: float32 [512, 512], replicated, may hold values from -0.25 to 0.25
- w_out: float32 [512, 512], replicated, may hold values from -0.25 to 0.25
- grad_attended: float32 [8, 4096, 512], P('dp', 'seq'), may hold values from -6 to 6
Outputs:
- attended: float32 [8, 4096, 512], P('dp', 'seq')
- grad_query_w: float32 [512, 512], replicated
- grad_key_w: float32 [512, 512], replicated
- grad_value_w: float32 [512, 512], replicated
- grad_out_w: float32 [512, 512], replicated
- grad_table: float32 [4096, 512], P(('dp', 'seq'))
The draws below stay inside these ranges and needn't reach their ends.
Inputs may be any that keep to these rules, and one draw needn't show every extreme that they name: `serve_lists`: within each list of 128 the entries are distinct rows of the owner's shard. `event_slots`: A slot s names entry s % 128 of the list that shard s // 128 serves to the event's device. On every device, for some shard, all 128 entries of its list are named by events. `session_tiles`: tile (i, i) is 1 for every i.
All inputs are finite; a program needn't handle non-finite values.
Results may differ from the reference program's by a relative error of at most 0.0003.
Values sent between devices are 32-bit elements; how exact they have to be, the bound alone decides.
No kernel may reach another device: no remote copies, remote signals or barrier semaphores. Data moves between devices by JAX's collectives and lax.ppermute only.
A program may use at most 192 MiB of HBM per device.

```python
import math
import jax
import jax.numpy as jnp
from jax import lax

D = 512
HEADS = 8
HEAD_DIM = 64
TILE = 128
TOK_DEV = 256
ROWS_SHARD = 512
HIST = 4096
TABLE = 4096
N_DP = 8
N_SEQ = 16


def shard_orders(key):
    keys = jax.random.split(jax.random.fold_in(key, 11), N_DP)
    return jax.vmap(lambda single: jax.random.permutation(single, ROWS_SHARD))(keys).astype(jnp.int32)


def serving_plan(key):
    orders = shard_orders(key)
    base = jax.random.fold_in(key, 23)
    devices = N_DP * N_SEQ
    ranking = jax.random.permutation(jax.random.fold_in(base, 1), devices).astype(jnp.int32)
    random_full = jax.random.randint(jax.random.fold_in(base, 2), (devices,), 0, N_DP)
    full_owner = jnp.where(ranking < N_DP, ranking, random_full)
    lowest = TILE * 7 // 32
    highest = TILE * 11 // 32 + 1
    counts = jax.random.randint(jax.random.fold_in(base, 3), (devices, N_DP), lowest, highest)
    counts = jnp.where(jnp.arange(N_DP)[None, :] == full_owner[:, None], TILE, counts).astype(jnp.int32)
    list_keys = jax.random.split(jax.random.fold_in(base, 4), N_DP * devices)
    picks = jax.vmap(lambda single: jax.random.permutation(single, ROWS_SHARD - 4)[:TILE - 4])(list_keys)
    picks = picks.reshape(N_DP, N_DP, N_SEQ, TILE - 4).astype(jnp.int32) + 4
    leading = jnp.broadcast_to(jnp.arange(4, dtype=jnp.int32), (N_DP, N_DP, N_SEQ, 4))
    positions = jnp.concatenate([leading, picks], axis=3)
    owner_index = jnp.arange(N_DP, dtype=jnp.int32)[:, None, None, None]
    lists = orders[owner_index, positions]
    event_keys = jax.random.split(jax.random.fold_in(base, 5), devices)

    def device_slots(single, count_row):
        total = jnp.sum(count_row)
        ordering = jax.random.permutation(jax.random.fold_in(single, 1), 2 * TOK_DEV).astype(jnp.int32)
        extra = jax.random.randint(jax.random.fold_in(single, 2), (2 * TOK_DEV,), 0, total)
        flat = jnp.where(ordering < total, ordering, extra)
        ends = jnp.cumsum(count_row)
        owners = jnp.sum((flat[:, None] >= ends[None, :]).astype(jnp.int32), axis=1)
        starts = ends - count_row
        return owners * TILE + flat - starts[owners]
    slots = jax.vmap(device_slots)(event_keys, counts)
    slots = slots.reshape(N_DP, N_SEQ, 2, TOK_DEV).transpose(0, 2, 1, 3).reshape(N_DP, 2, N_SEQ * TOK_DEV)
    return (lists.astype(jnp.int32), slots.astype(jnp.int32))


def draw_serve_lists(key, part):
    plan = serving_plan(key)
    return plan[0]


def draw_event_slots(key, part):
    plan = serving_plan(key)
    return plan[1]


def draw_item_table(key, part):
    key = jax.random.fold_in(key, 41)
    return jnp.clip(jax.random.normal(jax.random.fold_in(key, 1), (TABLE, D)), -6.0, 6.0)


def projection_pair(key):
    first = jnp.clip(jax.random.normal(jax.random.fold_in(key, 51), (D, D)), -5.0, 5.0)
    second = jnp.clip(jax.random.normal(jax.random.fold_in(key, 52), (D, D)), -5.0, 5.0)
    return (first, second)


def draw_w_query(key, part):
    first, second = projection_pair(key)
    return first * D ** (-0.5)


def draw_w_key(key, part):
    first, second = projection_pair(key)
    return second * D ** (-0.5)


def draw_session_tiles(key, part):
    key = jax.random.fold_in(key, 71)
    tiles = HIST // TILE
    per_device = TOK_DEV // TILE
    levels = jax.random.randint(jax.random.fold_in(key, 1), (N_DP, N_SEQ, 1, 1), 1, 10)
    levels = jnp.broadcast_to(levels, (N_DP, N_SEQ, per_device, tiles)).reshape(N_DP, tiles, tiles)
    coins = jax.random.randint(jax.random.fold_in(key, 2), (N_DP, tiles, tiles), 0, 10)
    diagonal = jnp.eye(tiles, dtype=jnp.int32)[None]
    return jnp.maximum((coins < levels).astype(jnp.int32), diagonal)


def block_scale(stream_key, shape, cuts, least, high):
    def one(position, blocks):
        heights = jax.random.uniform(jax.random.fold_in(jax.random.fold_in(stream_key, 6), position), (blocks,), jnp.float32, least / len(cuts), high / len(cuts))
        return jnp.repeat(jnp.exp(heights), shape[position] // blocks).reshape((-1,) + (1,) * (len(shape) - position - 1))

    gain = one(*cuts[0])
    for cut in cuts[1:]:
        gain = gain * one(*cut)
    return gain


def bell_draw(rng, shape, deviation, bound, pieces=(), kind=jnp.bfloat16):
    values = deviation * jax.random.normal(rng, shape, jnp.float32)
    if pieces:
        values = values * block_scale(rng, shape, pieces, -0.22, 0.18)
    return jnp.clip(values, -bound, bound).astype(kind)


def setup_inputs(seed: int = 0) -> dict:
    streams_of = jax.random.split(jax.random.key(seed), 10)
    return {
        "item_table": draw_item_table(jax.random.fold_in(streams_of[9], 71), 0),
        "serve_lists": draw_serve_lists(jax.random.fold_in(streams_of[9], 71), 0),
        "event_slots": draw_event_slots(jax.random.fold_in(streams_of[9], 71), 0),
        "session_tiles": draw_session_tiles(jax.random.fold_in(streams_of[9], 71), 0),
        "w_query": draw_w_query(jax.random.fold_in(streams_of[9], 71), 0),
        "w_key": draw_w_key(jax.random.fold_in(streams_of[9], 71), 0),
        "w_value": bell_draw(streams_of[6], (D, D), D ** -0.5, 0.25, (), jnp.float32),
        "w_out": bell_draw(streams_of[7], (D, D), D ** -0.5, 0.25, (), jnp.float32),
        "grad_attended": bell_draw(streams_of[8], (N_DP, HIST, D), 1.0, 6.0, ((0, 8), (1, 16)), jnp.float32),
    }


HIGH = lax.Precision.HIGHEST
NEGATIVE = -1e30


def product(left, right):
    return jnp.dot(left, right, precision=HIGH, preferred_element_type=jnp.float32)


def gather_inputs(item_table, serve_lists, event_slots):
    owners = event_slots // TILE
    within = event_slots % TILE
    users = jnp.arange(N_DP, dtype=jnp.int32)[:, None, None]
    blocks = (jnp.arange(HIST, dtype=jnp.int32) // TOK_DEV)[None, None, :]
    local = serve_lists[owners, users, blocks, within]
    table_rows = owners * ROWS_SHARD + local
    picked = item_table[table_rows]
    return picked[:, 0] + picked[:, 1], table_rows


def attend_user(inputs, tiles, cotangent, w_query, w_key, w_value, w_out):
    scale = HEAD_DIM ** -0.5
    queries = product(inputs, w_query).reshape(HIST, HEADS, HEAD_DIM)
    keys = product(inputs, w_key).reshape(HIST, HEADS, HEAD_DIM)
    values = product(inputs, w_value).reshape(HIST, HEADS, HEAD_DIM)
    block_rows = math.gcd(HIST, 512)
    block_count = HIST // block_rows
    block_tiles = block_rows // TILE

    def block_mask(index):
        tile_rows = lax.dynamic_slice_in_dim(tiles, index * block_tiles, block_tiles, 0)
        spread = jnp.broadcast_to(tile_rows[:, None, :, None], (block_tiles, TILE, HIST // TILE, TILE))
        return spread.reshape(block_rows, HIST) > 0

    def block_scores(index):
        block_queries = lax.dynamic_slice_in_dim(queries, index * block_rows, block_rows, 0)
        scores = jnp.einsum("qhd,khd->hqk", block_queries, keys, precision=HIGH) * scale
        mask = block_mask(index)
        return block_queries, mask, jnp.where(mask[None], scores, NEGATIVE)

    def forward_block(index):
        block_queries, mask, scores = block_scores(index)
        peak = jnp.max(scores, axis=2, keepdims=True)
        weights = jnp.exp(scores - peak) * mask[None]
        total = jnp.sum(weights, axis=2, keepdims=True)
        context = jnp.einsum("hqk,khd->qhd", weights / total, values, precision=HIGH)
        return context, (peak + jnp.log(total))[:, :, 0]

    indices = jnp.arange(block_count, dtype=jnp.int32)
    context, log_total = lax.map(forward_block, indices)
    context = context.reshape(HIST, D)
    log_total = log_total.transpose(1, 0, 2).reshape(HEADS, HIST)
    attended = product(context, w_out)
    grad_out_w = product(context.T, cotangent)
    grad_context = product(cotangent, w_out.T).reshape(HIST, HEADS, HEAD_DIM)
    delta = jnp.sum(grad_context * context.reshape(HIST, HEADS, HEAD_DIM), axis=2).T

    def backward_block(carry, index):
        grad_keys, grad_values = carry
        block_queries, mask, scores = block_scores(index)
        block_grad = lax.dynamic_slice_in_dim(grad_context, index * block_rows, block_rows, 0)
        block_total = lax.dynamic_slice_in_dim(log_total, index * block_rows, block_rows, 1)
        block_delta = lax.dynamic_slice_in_dim(delta, index * block_rows, block_rows, 1)
        probs = jnp.exp(scores - block_total[:, :, None]) * mask[None]
        grad_values = grad_values + jnp.einsum("hqk,qhd->khd", probs, block_grad, precision=HIGH)
        grad_probs = jnp.einsum("qhd,khd->hqk", block_grad, values, precision=HIGH)
        grad_scores = probs * (grad_probs - block_delta[:, :, None])
        block_grad_queries = jnp.einsum("hqk,khd->qhd", grad_scores, keys, precision=HIGH) * scale
        grad_keys = grad_keys + jnp.einsum("hqk,qhd->khd", grad_scores, block_queries, precision=HIGH) * scale
        return (grad_keys, grad_values), block_grad_queries

    zeros = jnp.zeros((HIST, HEADS, HEAD_DIM), jnp.float32)
    (grad_keys, grad_values), grad_queries = lax.scan(backward_block, (zeros, zeros), indices)
    grad_queries = grad_queries.reshape(HIST, D)
    grad_keys = grad_keys.reshape(HIST, D)
    grad_values = grad_values.reshape(HIST, D)
    grad_query_w = product(inputs.T, grad_queries)
    grad_key_w = product(inputs.T, grad_keys)
    grad_value_w = product(inputs.T, grad_values)
    grad_inputs = product(grad_queries, w_query.T) + product(grad_keys, w_key.T) + product(grad_values, w_value.T)
    return attended, grad_query_w, grad_key_w, grad_value_w, grad_out_w, grad_inputs


def reference(item_table, serve_lists, event_slots, session_tiles, w_query, w_key, w_value, w_out, grad_attended):
    inputs, table_rows = gather_inputs(item_table, serve_lists, event_slots)

    def one_user(packed):
        return attend_user(packed[0], packed[1], packed[2], w_query, w_key, w_value, w_out)

    attended, grad_q, grad_k, grad_v, grad_o, grad_inputs = lax.map(one_user, (inputs, session_tiles, grad_attended))
    spread = jnp.broadcast_to(grad_inputs[:, None], (N_DP, 2, HIST, D)).reshape(-1, D)
    grad_table = jnp.zeros((TABLE, D), jnp.float32).at[table_rows.reshape(-1)].add(spread)
    return (attended, jnp.sum(grad_q, axis=0), jnp.sum(grad_k, axis=0), jnp.sum(grad_v, axis=0),
            jnp.sum(grad_o, axis=0), grad_table)
```

```python
import jax
import jax.numpy as jnp
from jax import lax
from jax.experimental import pallas as pl
from jax.experimental.pallas import tpu as pltpu
from jax.sharding import PartitionSpec as P

HEADS = 8
HEAD_DIM = 64
TILE = 128
SPAN = 512
BF = jnp.bfloat16
F32 = jnp.float32
EXACT = lax.Precision.HIGHEST
THREE = lax.Precision.HIGH


def product(left, right, precision=THREE):
    return jnp.dot(left, right, precision=precision, preferred_element_type=F32)


def dot_nn(a, b):
    return lax.dot_general(a, b, (((1,), (0,)), ((), ())), preferred_element_type=F32)


def dot_tn(a, b):
    return lax.dot_general(a, b, (((0,), (0,)), ((), ())), preferred_element_type=F32)


def halves(x):
    hi = x.astype(BF)
    lo = (x - hi.astype(F32)).astype(BF)
    return hi, lo


def make(span):
    def kernel(bias, qt4, qs2, dot_, k_ref, v_ref, ctx_ref, dq_ref, dk_ref, dv_ref, k2, v2, s_ref, ph, plo):
        rows = k_ref.shape[0]
        nb = rows // span
        tiles = span // 128
        low = lax.broadcasted_iota(jnp.int32, (span, 128), 1) < 64
        for head in range(2):
            def prepare(i, c):
                at = pl.ds(pl.multiple_of(i * span, span), span)
                for src, dst in ((k_ref, k2), (v_ref, v2)):
                    x = src[at, :]
                    hi = x.astype(BF).astype(F32)
                    lo = x - hi
                    if head == 0:
                        both = jnp.where(low, hi, pltpu.roll(lo, 64, 1))
                    else:
                        both = jnp.where(low, pltpu.roll(hi, 64, 1), lo)
                    dst[at, :] = both.astype(BF)
                return c
            lax.fori_loop(0, nb, prepare, 0)
            q4 = qt4[head]

            def score(i, peak):
                at = pl.ds(pl.multiple_of(i * span, span), span)
                k = k2[at, :]
                s = dot_nn(jnp.concatenate([k, k], axis=1), q4)
                parts = []
                for t in range(tiles):
                    st = s[t * 128:(t + 1) * 128] + bias[pl.ds(i * tiles + t, 1), :]
                    s_ref[pl.ds(pl.multiple_of(i * span + t * 128, 128), 128), :] = st
                    peak = jnp.maximum(peak, jnp.max(st.reshape(16, 8, 256), axis=0))
                return peak
            peak = lax.fori_loop(0, nb, score, jnp.full((8, 256), -3e38, F32))
            peak = jnp.max(peak, axis=0, keepdims=True)

            def weigh(i, carry):
                total, acc = carry
                at = pl.ds(pl.multiple_of(i * span, span), span)
                p = jnp.exp2(s_ref[at, :] - peak)
                total = total + jnp.sum(p.reshape(span // 8, 8, 256), axis=0)
                hi, lo = halves(p)
                ph[at, :] = hi
                plo[at, :] = lo
                v = v2[at, :]
                acc = acc + dot_tn(v, hi) + dot_tn(v, lo)
                return total, acc
            total, acc = lax.fori_loop(0, nb, weigh, (jnp.zeros((8, 256), F32), jnp.zeros((128, 256), F32)))
            share = 1.0 / jnp.sum(total, axis=0, keepdims=True)
            ctx = (acc[:64] + acc[64:]) * share
            ctx_ref[head * 64:(head + 1) * 64, :] = ctx
            g = dot_[head] * share
            delta = jnp.sum(g * ctx, axis=0, keepdims=True)
            ghi = g.astype(BF).astype(F32)
            glo = g - ghi
            g2 = jnp.concatenate([ghi, glo], axis=0)
            g4 = jnp.concatenate([ghi, ghi, glo, glo], axis=0).astype(BF)
            gn = g2.T.astype(BF)
            qn = qs2[head]

            def back(i, acc):
                at = pl.ds(pl.multiple_of(i * span, span), span)
                v = v2[at, :]
                k = k2[at, :]
                dp = dot_nn(jnp.concatenate([v, v], axis=1), g4)
                hi = ph[at, :]
                lo = plo[at, :]
                ds = (hi.astype(F32) + lo.astype(F32)) * (dp - delta)
                dv = dot_nn(hi, gn) + dot_nn(lo, gn)
                dv = dv + pltpu.roll(dv, 64, 1)
                shi, slo = halves(ds)
                dk = dot_nn(shi, qn) + dot_nn(slo, qn)
                dk = dk + pltpu.roll(dk, 64, 1)
                if head == 0:
                    dv_ref[at, :] = dv
                    dk_ref[at, :] = dk
                else:
                    dv_ref[at, :] = jnp.where(low, dv_ref[at, :], dv)
                    dk_ref[at, :] = jnp.where(low, dk_ref[at, :], dk)
                return acc + dot_tn(k, shi) + dot_tn(k, slo)
            acc = lax.fori_loop(0, nb, back, jnp.zeros((128, 256), F32))
            dq_ref[head * 64:(head + 1) * 64, :] = acc[:64] + acc[64:]

    def call(bias, qt4, qs2, dot_, kv):
        rows = kv.shape[0]
        pairs = 4
        return pl.pallas_call(
            kernel,
            grid=(pairs,),
            in_specs=[
                pl.BlockSpec(bias.shape, lambda p: (0, 0)),
                pl.BlockSpec((2, 256, 256), lambda p: (p, 0, 0)),
                pl.BlockSpec((2, 256, 128), lambda p: (p, 0, 0)),
                pl.BlockSpec((2, 64, 256), lambda p: (p, 0, 0)),
                pl.BlockSpec((rows, 128), lambda p: (0, p)),
                pl.BlockSpec((rows, 128), lambda p: (0, 4 + p)),
            ],
            out_specs=[
                pl.BlockSpec((128, 256), lambda p: (p, 0)),
                pl.BlockSpec((128, 256), lambda p: (p, 0)),
                pl.BlockSpec((rows, 128), lambda p: (0, p)),
                pl.BlockSpec((rows, 128), lambda p: (0, p)),
            ],
            out_shape=[
                jax.ShapeDtypeStruct((512, 256), F32),
                jax.ShapeDtypeStruct((512, 256), F32),
                jax.ShapeDtypeStruct((rows, 512), F32),
                jax.ShapeDtypeStruct((rows, 512), F32),
            ],
            scratch_shapes=[
                pltpu.VMEM((rows, 128), BF),
                pltpu.VMEM((rows, 128), BF),
                pltpu.VMEM((rows, 256), F32),
                pltpu.VMEM((rows, 256), BF),
                pltpu.VMEM((rows, 256), BF),
            ],
            compiler_params=pltpu.CompilerParams(vmem_limit_bytes=56 * 1024 * 1024),
        )(bias, qt4, qs2, dot_, kv, kv)
    return call

def split_xla(x):
    hi = lax.reduce_precision(x, 8, 7)
    return hi, x - hi

def operands(q, dctx, tiles):
    log2e = 1.4426950408889634
    qt = (q * log2e).T.reshape(8, 64, 256)
    hi, lo = split_xla(qt)
    qt4 = jnp.concatenate([hi, hi, lo, lo], axis=1).astype(BF)
    qh = q.reshape(256, 8, 64).transpose(1, 0, 2)
    hi, lo = split_xla(qh)
    qs2 = jnp.concatenate([hi, lo], axis=2).astype(BF)
    dot_ = dctx.T.reshape(8, 64, 256)
    bias = jnp.where(tiles.T > 0, 0.0, -1e30).astype(F32)
    bias = jnp.repeat(bias, 128, axis=1)
    return bias, qt4, qs2, dot_


def on_device(
    item_table,
    serve_lists,
    event_slots,
    session_tiles,
    w_query,
    w_key,
    w_value,
    w_out,
    grad_attended,
):
    width = item_table.shape[1]
    lists = serve_lists[0, :, 0, :]
    served = item_table[lists]
    arrived = lax.all_to_all(served, "dp", split_axis=0, concat_axis=0, tiled=True)
    slot_rows = arrived.reshape(-1, width)
    slots = event_slots[0]
    inputs = slot_rows[slots[0]] + slot_rows[slots[1]]
    history = lax.all_gather(inputs, "seq", axis=0, tiled=True)
    cotangent = grad_attended[0]
    scale = HEAD_DIM ** (-0.5)
    queries = product(inputs, w_query, EXACT) * scale
    grad_context = product(cotangent, w_out.T)
    w_both = jnp.concatenate([w_key, w_value], axis=1)
    both = product(history, w_both)
    context_t, grad_queries_t, grad_keys, grad_values = make(SPAN)(
        *operands(queries, grad_context, session_tiles[0]), both
    )
    context = context_t.T
    grad_queries = grad_queries_t.T * scale
    attended = product(context, w_out)
    grad_out_w = product(context_t, cotangent)
    grad_query_w = product(inputs.T, grad_queries)
    grad_key_w = product(history.T, grad_keys)
    grad_value_w = product(history.T, grad_values)
    partial = product(grad_keys, w_key.T) + product(grad_values, w_value.T)
    grad_inputs = lax.psum_scatter(partial, "seq", scatter_dimension=0, tiled=True)
    grad_inputs = grad_inputs + product(grad_queries, w_query.T)
    doubled = jnp.concatenate([grad_inputs, grad_inputs], axis=0)
    slot_grads = jax.ops.segment_sum(
        doubled, jnp.concatenate([slots[0], slots[1]]), num_segments=slot_rows.shape[0]
    )
    returned = lax.all_to_all(
        slot_grads.reshape(arrived.shape), "dp", split_axis=0, concat_axis=0, tiled=True
    )
    table_terms = jax.ops.segment_sum(
        returned.reshape(-1, width), lists.reshape(-1), num_segments=item_table.shape[0]
    )
    grad_table = lax.psum_scatter(table_terms, "seq", scatter_dimension=0, tiled=True)
    grad_query_w, grad_key_w, grad_value_w, grad_out_w = lax.psum(
        (grad_query_w, grad_key_w, grad_value_w, grad_out_w), ("dp", "seq")
    )
    return (attended[None], grad_query_w, grad_key_w, grad_value_w, grad_out_w, grad_table)


def solution(mesh):
    return jax.shard_map(
        on_device,
        mesh=mesh,
        in_specs=(
            P("dp", None),
            P("dp", None, "seq", None),
            P("dp", None, "seq"),
            P("dp", "seq", None),
            P(),
            P(),
            P(),
            P(),
            P("dp", "seq", None),
        ),
        out_specs=(P("dp", "seq", None), P(), P(), P(), P(), P(("dp", "seq"), None)),
        check_vma=False,
    )
```

```python
import jax
import jax.numpy as jnp
from jax import lax
from jax.experimental import pallas as pl
from jax.experimental.pallas import tpu as pltpu
from jax.sharding import Mesh, PartitionSpec as P

HEADS = 8
HEAD_DIM = 64
TILE = 128
SPAN = 512
MIB = 1024 * 1024
BF = jnp.bfloat16
F32 = jnp.float32
EXACT = lax.Precision.HIGHEST
THREE = lax.Precision.HIGH


def product(left, right, precision=THREE):
    return jnp.dot(left, right, precision=precision, preferred_element_type=F32)

def dot_nn(a, b):
    return lax.dot_general(a, b, (((1,), (0,)), ((), ())), preferred_element_type=F32)

def dot_tn(a, b):
    return lax.dot_general(a, b, (((0,), (0,)), ((), ())), preferred_element_type=F32)

def halves(x):
    hi = x.astype(BF)
    lo = (x - hi.astype(F32)).astype(BF)
    return hi, lo

def make(span):
    def kernel(bias, qt4, qs2, dot_, k_ref, v_ref, ctx_ref, dq_ref, dk_ref, dv_ref, k2, v2, s_ref, ph, plo):
        rows = k_ref.shape[0]
        nb = rows // span
        tiles = span // 128
        low = lax.broadcasted_iota(jnp.int32, (span, 128), 1) < 64
        for head in range(2):
            def prepare(i, c):
                at = pl.ds(pl.multiple_of(i * span, span), span)
                for src, dst in ((k_ref, k2), (v_ref, v2)):
                    x = src[at, :]
                    hi = x.astype(BF).astype(F32)
                    lo = x - hi
                    if head == 0:
                        both = jnp.where(low, hi, pltpu.roll(lo, 64, 1))
                    else:
                        both = jnp.where(low, pltpu.roll(hi, 64, 1), lo)
                    dst[at, :] = both.astype(BF)
                return c
            lax.fori_loop(0, nb, prepare, 0)
            q4 = qt4[head]

            def score(i, peak):
                at = pl.ds(pl.multiple_of(i * span, span), span)
                k = k2[at, :]
                s = dot_nn(jnp.concatenate([k, k], axis=1), q4)
                parts = []
                for t in range(tiles):
                    st = s[t * 128:(t + 1) * 128] + bias[pl.ds(i * tiles + t, 1), :]
                    s_ref[pl.ds(pl.multiple_of(i * span + t * 128, 128), 128), :] = st
                    peak = jnp.maximum(peak, jnp.max(st.reshape(16, 8, 256), axis=0))
                return peak
            peak = lax.fori_loop(0, nb, score, jnp.full((8, 256), -3e38, F32))
            peak = jnp.max(peak, axis=0, keepdims=True)

            def weigh(i, carry):
                total, acc = carry
                at = pl.ds(pl.multiple_of(i * span, span), span)
                p = jnp.exp2(s_ref[at, :] - peak)
                total = total + jnp.sum(p.reshape(span // 8, 8, 256), axis=0)
                hi, lo = halves(p)
                ph[at, :] = hi
                plo[at, :] = lo
                v = v2[at, :]
                acc = acc + dot_tn(v, hi) + dot_tn(v, lo)
                return total, acc
            total, acc = lax.fori_loop(0, nb, weigh, (jnp.zeros((8, 256), F32), jnp.zeros((128, 256), F32)))
            share = 1.0 / jnp.sum(total, axis=0, keepdims=True)
            ctx = (acc[:64] + acc[64:]) * share
            ctx_ref[head * 64:(head + 1) * 64, :] = ctx
            g = dot_[head] * share
            delta = jnp.sum(g * ctx, axis=0, keepdims=True)
            ghi = g.astype(BF).astype(F32)
            glo = g - ghi
            g2 = jnp.concatenate([ghi, glo], axis=0)
            g4 = jnp.concatenate([ghi, ghi, glo, glo], axis=0).astype(BF)
            gn = g2.T.astype(BF)
            qn = qs2[head]

            def back(i, acc):
                at = pl.ds(pl.multiple_of(i * span, span), span)
                v = v2[at, :]
                k = k2[at, :]
                dp = dot_nn(jnp.concatenate([v, v], axis=1), g4)
                hi = ph[at, :]
                lo = plo[at, :]
                ds = (hi.astype(F32) + lo.astype(F32)) * (dp - delta)
                dv = dot_nn(hi, gn) + dot_nn(lo, gn)
                dv = dv + pltpu.roll(dv, 64, 1)
                shi, slo = halves(ds)
                dk = dot_nn(shi, qn) + dot_nn(slo, qn)
                dk = dk + pltpu.roll(dk, 64, 1)
                if head == 0:
                    dv_ref[at, :] = dv
                    dk_ref[at, :] = dk
                else:
                    dv_ref[at, :] = jnp.where(low, dv_ref[at, :], dv)
                    dk_ref[at, :] = jnp.where(low, dk_ref[at, :], dk)
                return acc + dot_tn(k, shi) + dot_tn(k, slo)
            acc = lax.fori_loop(0, nb, back, jnp.zeros((128, 256), F32))
            dq_ref[head * 64:(head + 1) * 64, :] = acc[:64] + acc[64:]

    def call(bias, qt4, qs2, dot_, kv):
        rows = kv.shape[0]
        pairs = 4
        return pl.pallas_call(
            kernel,
            grid=(pairs,),
            in_specs=[
                pl.BlockSpec(bias.shape, lambda p: (0, 0)),
                pl.BlockSpec((2, 256, 256), lambda p: (p, 0, 0)),
                pl.BlockSpec((2, 256, 128), lambda p: (p, 0, 0)),
                pl.BlockSpec((2, 64, 256), lambda p: (p, 0, 0)),
                pl.BlockSpec((rows, 128), lambda p: (0, p)),
                pl.BlockSpec((rows, 128), lambda p: (0, 4 + p)),
            ],
            out_specs=[
                pl.BlockSpec((128, 256), lambda p: (p, 0)),
                pl.BlockSpec((128, 256), lambda p: (p, 0)),
                pl.BlockSpec((rows, 128), lambda p: (0, p)),
                pl.BlockSpec((rows, 128), lambda p: (0, p)),
            ],
            out_shape=[
                jax.ShapeDtypeStruct((512, 256), F32),
                jax.ShapeDtypeStruct((512, 256), F32),
                jax.ShapeDtypeStruct((rows, 512), F32),
                jax.ShapeDtypeStruct((rows, 512), F32),
            ],
            scratch_shapes=[
                pltpu.VMEM((rows, 128), BF),
                pltpu.VMEM((rows, 128), BF),
                pltpu.VMEM((rows, 256), F32),
                pltpu.VMEM((rows, 256), BF),
                pltpu.VMEM((rows, 256), BF),
            ],
            compiler_params=pltpu.CompilerParams(vmem_limit_bytes=56 * 1024 * 1024),
        )(bias, qt4, qs2, dot_, kv, kv)
    return call

def split_xla(x):
    hi = lax.reduce_precision(x, 8, 7)
    return hi, x - hi

def operands(q, dctx, tiles):
    log2e = 1.4426950408889634
    qt = (q * log2e).T.reshape(8, 64, 256)
    hi, lo = split_xla(qt)
    qt4 = jnp.concatenate([hi, hi, lo, lo], axis=1).astype(BF)
    qh = q.reshape(256, 8, 64).transpose(1, 0, 2)
    hi, lo = split_xla(qh)
    qs2 = jnp.concatenate([hi, lo], axis=2).astype(BF)
    dot_ = dctx.T.reshape(8, 64, 256)
    bias = jnp.where(tiles.T > 0, 0.0, -1e30).astype(F32)
    bias = jnp.repeat(bias, 128, axis=1)
    return bias, qt4, qs2, dot_


def front(pieces, slots, w_hi, w_lo, rows, span=512, unroll=8):
    width = 512
    n = len(pieces)
    count = sum(p.shape[0] for p in pieces)
    def kernel(*refs):
        idx = refs[0]
        parts = refs[1:1 + n]
        wh, wl, x_ref, kv_ref, table, flat, sem = refs[1 + n:]
        step = pl.program_id(0)
        @pl.when(step == 0)
        def _():
            copies = []
            at = 0
            for j, p in enumerate(parts):
                copies.append(pltpu.make_async_copy(p, table.at[pl.ds(at, p.shape[0])], sem.at[j]))
                at += p.shape[0]
            for c in copies:
                c.start()
            for c in copies:
                c.wait()
        def body(i, c):
            for u in range(unroll):
                e = i * unroll + u
                a = idx[0, step * span + e]
                b = idx[1, step * span + e]
                a = pl.multiple_of(a * 4, 4)
                b = pl.multiple_of(b * 4, 4)
                flat[pl.ds(pl.multiple_of(e * 4, 4), 4), :] = table[pl.ds(a, 4), :] + table[pl.ds(b, 4), :]
            return c
        lax.fori_loop(0, span // unroll, body, 0)
        x = jnp.concatenate([flat[pl.ds(j, span, stride=4), :] for j in range(4)], axis=1)
        x_ref[...] = x
        hi, lo = halves(x)
        kv_ref[...] = dot_nn(hi, wh[...]) + dot_nn(hi, wl[...]) + dot_nn(lo, wh[...])
    return pl.pallas_call(
        kernel,
        grid=(rows // span,),
        in_specs=[pl.BlockSpec(memory_space=pltpu.SMEM)]
        + [pl.BlockSpec(memory_space=pl.ANY)] * n
        + [pl.BlockSpec(w_hi.shape, lambda i: (0, 0))] * 2,
        out_specs=[pl.BlockSpec((span, width), lambda i: (i, 0)), pl.BlockSpec((span, 2 * width), lambda i: (i, 0))],
        out_shape=[jax.ShapeDtypeStruct((rows, width), F32), jax.ShapeDtypeStruct((rows, 2 * width), F32)],
        scratch_shapes=[pltpu.VMEM((count, 128), F32), pltpu.VMEM((span * 4, 128), F32), pltpu.SemaphoreType.DMA((n,))],
        compiler_params=pltpu.CompilerParams(vmem_limit_bytes=56 * MIB),
    )(slots, *pieces, w_hi, w_lo)

def back(slots, own, dk, dv, x, wt_hi, wt_lo, qx, count, span=512, unroll=8, chains=4):
    rows, width = x.shape
    def kernel(idx, own_ref, dk_ref, dv_ref, x_ref, wh, wl, qx_ref, acc, w_ref, *more):
        *others, dx, flat = more
        accs = [acc, *others]
        step = pl.program_id(0)
        @pl.when(step == 0)
        def _():
            w_ref[...] = jnp.zeros_like(w_ref)
            def clear(i, c):
                at = pl.ds(pl.multiple_of(i * 512, 512), 512)
                for a in accs:
                    a[at, :] = jnp.zeros((512, 128), F32)
                return c
            lax.fori_loop(0, count * 4 // 512, clear, 0)
        khi, klo = halves(dk_ref[...])
        vhi, vlo = halves(dv_ref[...])
        hi = jnp.concatenate([khi, vhi], axis=1)
        lo = jnp.concatenate([klo, vlo], axis=1)
        dx[...] = dot_nn(hi, wh[...]) + dot_nn(hi, wl[...]) + dot_nn(lo, wh[...])
        xhi, xlo = halves(x_ref[...])
        w_ref[...] += dot_tn(hi, xhi) + dot_tn(hi, xlo) + dot_tn(lo, xhi)
        @pl.when(own_ref[0] // 2 == step)
        def _():
            at = pl.ds(pl.multiple_of(own_ref[0] % 2 * 256, 256), 256)
            dx[at, :] += qx_ref[...]
        for j in range(4):
            flat[pl.ds(j, span, stride=4), :] = dx[:, j * 128:(j + 1) * 128]
        def body(i, c):
            for u in range(unroll):
                e = i * unroll + u
                a = pl.multiple_of(idx[0, step * span + e] * 4, 4)
                b = pl.multiple_of(idx[1, step * span + e] * 4, 4)
                row = flat[pl.ds(pl.multiple_of(e * 4, 4), 4), :]
                k = u % (chains // 2) * 2
                accs[k][pl.ds(a, 4), :] += row
                accs[k + 1][pl.ds(b, 4), :] += row
            return c
        lax.fori_loop(0, span // unroll, body, 0)
        @pl.when(step == rows // span - 1)
        def _():
            def add(i, c):
                at = pl.ds(pl.multiple_of(i * 512, 512), 512)
                acc[at, :] = sum(a[at, :] for a in accs)
                return c
            lax.fori_loop(0, count * 4 // 512, add, 0)
    return pl.pallas_call(
        kernel,
        grid=(rows // span,),
        in_specs=[pl.BlockSpec(memory_space=pltpu.SMEM)] * 2
        + [pl.BlockSpec((span, width), lambda i: (i, 0))] * 3
        + [pl.BlockSpec((2 * width, width), lambda i: (0, 0))] * 2
        + [pl.BlockSpec(qx.shape, lambda i: (0, 0))],
        out_specs=[pl.BlockSpec((count * 4, 128), lambda i: (0, 0), pipeline_mode=pl.Buffered(1)), pl.BlockSpec((2 * width, width), lambda i: (0, 0), pipeline_mode=pl.Buffered(1))],
        out_shape=[jax.ShapeDtypeStruct((count * 4, 128), F32), jax.ShapeDtypeStruct((2 * width, width), F32)],
        scratch_shapes=[pltpu.VMEM((count * 4, 128), F32)] * (chains - 1) + [pltpu.VMEM((span, width), F32), pltpu.VMEM((span * 4, 128), F32)],
        compiler_params=pltpu.CompilerParams(vmem_limit_bytes=56 * MIB),
    )(slots, own, dk, dv, x, wt_hi, wt_lo, qx)


Z = ("zl", "zh")
SIZES = {"x": 4, "y": 4, Z: 4, "c": 2}

def shift(v, axis, s):
    n = SIZES[axis]
    place = (lambda z: z % 2 * 2 + z // 2) if axis == Z else (lambda i: i)
    return lax.ppermute(v, axis, [(place(i), place((i + s) % n)) for i in range(n)])

def ring_gather(v, axis):
    n = v.shape[0] // 2
    before = shift(v, axis, 1)
    after = shift(v, axis, -1)
    far_a = shift(before[:n], axis, 1)
    far_b = shift(after[n:], axis, -1)
    return [v, before, after, far_a, far_b]

def table_gather(shard):
    c = lax.axis_index("c")
    half = shard.shape[0] // 2
    mine = lax.dynamic_slice_in_dim(shard, c * half, half, 0)
    a1, a2 = mine[:half // 2], mine[half // 2:]
    q = half // 4
    za = shift(a2[:q], Z, 1)
    zb = shift(a2[q:], Z, -1)
    s1 = ring_gather(a1, "x")
    v2 = jnp.concatenate([a2, za, zb], 0)
    s2 = ring_gather(v2, "x")
    z1 = shift(jnp.concatenate(s1[:2], 0), Z, 1)
    z2 = shift(jnp.concatenate(s1[2:], 0), Z, -1)
    first = jnp.concatenate(s1 + [z1, z2], 0)
    other_first = shift(first, "c", 1)
    second = jnp.concatenate(s2, 0)
    other_second = shift(second, "c", 1)
    return first, second, other_first, other_second

def ring_scatter(v, axis):
    m = v.shape[0] // 4
    h = m // 2
    up = shift(v[m + h:2 * m + h], axis, 1)
    down = shift(v[2 * m + h:3 * m + h], axis, -1)
    up2 = shift(v[m:m + h] + up[h:], axis, 1)
    down2 = shift(v[3 * m + h:] + down[:h], axis, -1)
    top = v[:h] + down[h:] + up2
    low = v[h:m] + up[:h] + down2
    return jnp.concatenate([top, low], 0)

def direct_scatter(v, axis):
    m = v.shape[0] // 4
    a = shift(v[m:2 * m], axis, 1)
    b = shift(v[3 * m:], axis, -1)
    d = shift(v[2 * m:3 * m], axis, 2)
    return v[:m] + a + b + d

def scatter_parts(parts, orders, direct=True):
    out = []
    for v, order in zip(parts, orders):
        half = v.shape[0] // 2
        v = v[:half] + shift(v[half:], "c", 1)
        v = ring_scatter(v, order[0])
        for ax in order[1:]:
            v = direct_scatter(v, ax) if direct else ring_scatter(v, ax)
        out.append(v)
    return out

def direct_gather(v, axis):
    return jnp.concatenate([v, shift(v, axis, -1), shift(v, axis, 2), shift(v, axis, 1)], 0)

def ring_gather4(v, axis):
    own, before, after, fa, fb = ring_gather(v, axis)
    return jnp.concatenate([own, after, fa, fb, before], 0)

def gather_parts(parts, orders):
    out = []
    for v, order in zip(parts, orders):
        for ax in order[:0:-1]:
            v = direct_gather(v, ax)
        v = ring_gather4(v, order[0])
        out.append(jnp.concatenate([v, shift(v, "c", 1)], 0))
    return out


def coordinates():
    zl, x, y, zh, c = (lax.axis_index(a) for a in ("zl", "x", "y", "zh", "c"))
    return {"x": x, "y": y, Z: zh * 2 + zl, "c": c, "zl": zl, "zh": zh}


def table_place(row, me):
    owner, local = row // 512, row % 512
    half, part, within = local // 256, local % 256 // 128, local % 128
    turn = (owner % 4 - me["x"]) % 4
    order = jnp.where(turn == 0, 0, jnp.where(turn == 3, 1, jnp.where(turn == 1, 2, 3)))
    other = (owner // 4 != me["zl"]).astype(jnp.int32)
    first = other * 512 + order * 128 + within
    second = 1024 + order * 256 + other * 128 + within
    return jnp.where(half != me["c"], 2048, 0) + jnp.where(part == 0, first, second)


PARTS = (("x", "y", Z), ("y", Z, "x"), (Z, "x", "y"))
PART_ROWS = (16, 8, 8)


def scatter_place(row, me):
    owner, local = row // 512, row % 512
    seq, within = local // 32, local % 32
    at = {"x": owner % 4, "y": seq // 4, Z: seq // 2 % 2 * 2 + owner // 4, "c": seq % 2}
    turn = {k: (v - me[k]) % SIZES[k] for k, v in at.items()}
    result, base, low = jnp.zeros_like(row), 0, 0
    for order, n in zip(PARTS, PART_ROWS):
        block = turn["c"]
        for axis in order:
            block = block * 4 + turn[axis]
        place = base + block * n + within - low
        result = jnp.where((within >= low) & (within < low + n), place, result)
        base, low = base + 128 * n, low + n
    return result


def turned(order, me, back):
    ids = jnp.arange(128, dtype=jnp.int32)
    digits = [("c", ids // 64, 2), (order[0], ids // 16 % 4, 4), (order[1], ids // 4 % 4, 4), (order[2], ids % 4, 4)]
    out = jnp.zeros_like(ids)
    for axis, digit, n in digits:
        out = out * n + ((digit - me[axis]) if back else (digit + me[axis])) % n
    return out


def sum_everywhere(arrays, me):
    orders = PARTS[:2]
    sent = [v.reshape(128, 8, 512)[turned(o, me, False)].reshape(1024, 512) for v, o in zip(arrays, orders)]
    got = gather_parts(scatter_parts(sent, orders), orders)
    return [v.reshape(128, 8, 512)[turned(o, me, True)].reshape(1024, 512) for v, o in zip(got, orders)]


DP = ("zl", "x")
SEQ = ("y", "zh", "c")


def on_device(
    item_table,
    serve_lists,
    event_slots,
    session_tiles,
    w_query,
    w_key,
    w_value,
    w_out,
    grad_attended,
):
    me = coordinates()
    seq = lax.axis_index(SEQ)
    pieces = table_gather(item_table.reshape(-1, 128))
    lists = lax.all_to_all(serve_lists[0, :, 0, :], DP, split_axis=0, concat_axis=0, tiled=True)
    slots = event_slots[0]
    rows = slots // TILE * 512 + lists.reshape(-1)[slots]
    rows = lax.all_to_all(
        jnp.broadcast_to(rows.reshape(1, 4, 128), (16, 4, 128)), SEQ, split_axis=0, concat_axis=0, tiled=True
    )
    rows = rows.reshape(16, 2, 256).transpose(1, 0, 2).reshape(2, 4096)
    w_both = jnp.concatenate([w_key, w_value], axis=1)
    w_hi, w_lo = split_xla(w_both)
    w_hi, w_lo = w_hi.astype(BF), w_lo.astype(BF)
    history, both = front(pieces, table_place(rows, me), w_hi, w_lo, 4096)
    inputs = lax.dynamic_slice_in_dim(history, seq * 256, 256, 0)
    cotangent = grad_attended[0]
    scale = HEAD_DIM ** (-0.5)
    queries = product(inputs, w_query, EXACT) * scale
    grad_context = product(cotangent, w_out.T)
    context_t, grad_queries_t, grad_keys, grad_values = make(SPAN)(
        *operands(queries, grad_context, session_tiles[0]), both
    )
    context = context_t.T
    grad_queries = grad_queries_t.T * scale
    attended = product(context, w_out)
    grad_out_w = product(context_t, cotangent)
    grad_query_w = product(inputs.T, grad_queries)
    query_terms = product(grad_queries, w_query.T)
    terms, grad_both_w = back(
        scatter_place(rows, me), seq.reshape(1), grad_keys, grad_values, history, w_hi.T, w_lo.T, query_terms, 4096
    )
    sums = sum_everywhere([grad_both_w, jnp.concatenate([grad_query_w, grad_out_w], axis=0)], me)
    grad_key_w, grad_value_w = sums[0][:512].T, sums[0][512:].T
    grad_query_w, grad_out_w = sums[1][:512], sums[1][512:]
    cuts, at = [], 0
    for n in PART_ROWS:
        cuts.append(terms[at * 512:(at + n) * 512])
        at += n
    grad_table = jnp.concatenate(scatter_parts(cuts, PARTS), axis=0).reshape(32, 512)
    return (attended[None], grad_query_w, grad_key_w, grad_value_w, grad_out_w, grad_table)


def solution(mesh):
    fine = Mesh(mesh.devices.reshape(2, 4, 4, 2, 2), ("zl", "x", "y", "zh", "c"))
    return jax.shard_map(
        on_device,
        mesh=fine,
        in_specs=(
            P(DP, None),
            P(DP, None, SEQ, None),
            P(DP, None, SEQ),
            P(DP, SEQ, None),
            P(),
            P(),
            P(),
            P(),
            P(DP, SEQ, None),
        ),
        out_specs=(P(DP, SEQ, None), P(), P(), P(), P(), P(DP + SEQ, None)),
        check_vma=False,
    )
```

```python
import jax
import jax.numpy as jnp
from jax import lax
from jax.experimental import pallas as pl
from jax.experimental.pallas import tpu as pltpu
from jax.sharding import Mesh, PartitionSpec as P

HEADS = 8
HEAD_DIM = 64
TILE = 128
SPAN = 512
MIB = 1024 * 1024
BF = jnp.bfloat16
F32 = jnp.float32
EXACT = lax.Precision.HIGHEST
THREE = lax.Precision.HIGH


def product(left, right, precision=THREE):
    return jnp.dot(left, right, precision=precision, preferred_element_type=F32)

def dot_nn(a, b):
    return lax.dot_general(a, b, (((1,), (0,)), ((), ())), preferred_element_type=F32)

def dot_tn(a, b):
    return lax.dot_general(a, b, (((0,), (0,)), ((), ())), preferred_element_type=F32)

def halves(x):
    hi = x.astype(BF)
    lo = (x - hi.astype(F32)).astype(BF)
    return hi, lo

def make(span):
    def kernel(bias, qt4, qs2, dot_, k_ref, v_ref, ctx_ref, dq_ref, dk_ref, dv_ref, k2, v2, s_ref, ph, plo):
        rows = k_ref.shape[0]
        nb = rows // span
        tiles = span // 128
        low = lax.broadcasted_iota(jnp.int32, (span, 128), 1) < 64
        for head in range(2):
            def prepare(i, c):
                at = pl.ds(pl.multiple_of(i * span, span), span)
                for src, dst in ((k_ref, k2), (v_ref, v2)):
                    x = src[at, :]
                    hi = x.astype(BF).astype(F32)
                    lo = x - hi
                    if head == 0:
                        both = jnp.where(low, hi, pltpu.roll(lo, 64, 1))
                    else:
                        both = jnp.where(low, pltpu.roll(hi, 64, 1), lo)
                    dst[at, :] = both.astype(BF)
                return c
            lax.fori_loop(0, nb, prepare, 0)
            q4 = qt4[head]

            def score(i, peak):
                at = pl.ds(pl.multiple_of(i * span, span), span)
                k = k2[at, :]
                s = dot_nn(jnp.concatenate([k, k], axis=1), q4)
                parts = []
                for t in range(tiles):
                    st = s[t * 128:(t + 1) * 128] + bias[pl.ds(i * tiles + t, 1), :]
                    s_ref[pl.ds(pl.multiple_of(i * span + t * 128, 128), 128), :] = st
                    peak = jnp.maximum(peak, jnp.max(st.reshape(16, 8, 256), axis=0))
                return peak
            peak = lax.fori_loop(0, nb, score, jnp.full((8, 256), -3e38, F32))
            peak = jnp.max(peak, axis=0, keepdims=True)

            def weigh(i, carry):
                total, acc = carry
                at = pl.ds(pl.multiple_of(i * span, span), span)
                p = jnp.exp2(s_ref[at, :] - peak)
                total = total + jnp.sum(p.reshape(span // 8, 8, 256), axis=0)
                hi, lo = halves(p)
                ph[at, :] = hi
                plo[at, :] = lo
                v = v2[at, :]
                acc = acc + dot_tn(v, hi) + dot_tn(v, lo)
                return total, acc
            total, acc = lax.fori_loop(0, nb, weigh, (jnp.zeros((8, 256), F32), jnp.zeros((128, 256), F32)))
            share = 1.0 / jnp.sum(total, axis=0, keepdims=True)
            ctx = (acc[:64] + acc[64:]) * share
            ctx_ref[head * 64:(head + 1) * 64, :] = ctx
            g = dot_[head] * share
            delta = jnp.sum(g * ctx, axis=0, keepdims=True)
            ghi = g.astype(BF).astype(F32)
            glo = g - ghi
            g2 = jnp.concatenate([ghi, glo], axis=0)
            g4 = jnp.concatenate([ghi, ghi, glo, glo], axis=0).astype(BF)
            gn = g2.T.astype(BF)
            qn = qs2[head]

            def back(i, acc):
                at = pl.ds(pl.multiple_of(i * span, span), span)
                v = v2[at, :]
                k = k2[at, :]
                dp = dot_nn(jnp.concatenate([v, v], axis=1), g4)
                hi = ph[at, :]
                lo = plo[at, :]
                ds = (hi.astype(F32) + lo.astype(F32)) * (dp - delta)
                dv = dot_nn(hi, gn) + dot_nn(lo, gn)
                dv = dv + pltpu.roll(dv, 64, 1)
                shi, slo = halves(ds)
                dk = dot_nn(shi, qn) + dot_nn(slo, qn)
                dk = dk + pltpu.roll(dk, 64, 1)
                if head == 0:
                    dv_ref[at, :] = dv
                    dk_ref[at, :] = dk
                else:
                    dv_ref[at, :] = jnp.where(low, dv_ref[at, :], dv)
                    dk_ref[at, :] = jnp.where(low, dk_ref[at, :], dk)
                return acc + dot_tn(k, shi) + dot_tn(k, slo)
            acc = lax.fori_loop(0, nb, back, jnp.zeros((128, 256), F32))
            dq_ref[head * 64:(head + 1) * 64, :] = acc[:64] + acc[64:]

    def call(bias, qt4, qs2, dot_, kv):
        rows = kv.shape[0]
        pairs = 4
        return pl.pallas_call(
            kernel,
            grid=(pairs,),
            in_specs=[
                pl.BlockSpec(bias.shape, lambda p: (0, 0)),
                pl.BlockSpec((2, 256, 256), lambda p: (p, 0, 0)),
                pl.BlockSpec((2, 256, 128), lambda p: (p, 0, 0)),
                pl.BlockSpec((2, 64, 256), lambda p: (p, 0, 0)),
                pl.BlockSpec((rows, 128), lambda p: (0, p)),
                pl.BlockSpec((rows, 128), lambda p: (0, 4 + p)),
            ],
            out_specs=[
                pl.BlockSpec((128, 256), lambda p: (p, 0)),
                pl.BlockSpec((128, 256), lambda p: (p, 0)),
                pl.BlockSpec((rows, 128), lambda p: (0, p)),
                pl.BlockSpec((rows, 128), lambda p: (0, p)),
            ],
            out_shape=[
                jax.ShapeDtypeStruct((512, 256), F32),
                jax.ShapeDtypeStruct((512, 256), F32),
                jax.ShapeDtypeStruct((rows, 512), F32),
                jax.ShapeDtypeStruct((rows, 512), F32),
            ],
            scratch_shapes=[
                pltpu.VMEM((rows, 128), BF),
                pltpu.VMEM((rows, 128), BF),
                pltpu.VMEM((rows, 256), F32),
                pltpu.VMEM((rows, 256), BF),
                pltpu.VMEM((rows, 256), BF),
            ],
            compiler_params=pltpu.CompilerParams(vmem_limit_bytes=56 * MIB),
            cost_estimate=pl.CostEstimate(flops=90_000_000_000, bytes_accessed=32 * MIB, transcendentals=8 * MIB),
        )(bias, qt4, qs2, dot_, kv, kv)
    return call

def split_xla(x):
    hi = lax.reduce_precision(x, 8, 7)
    return hi, x - hi

def operands(q, dctx, tiles):
    log2e = 1.4426950408889634
    qt = (q * log2e).T.reshape(8, 64, 256)
    hi, lo = split_xla(qt)
    qt4 = jnp.concatenate([hi, hi, lo, lo], axis=1).astype(BF)
    qh = q.reshape(256, 8, 64).transpose(1, 0, 2)
    hi, lo = split_xla(qh)
    qs2 = jnp.concatenate([hi, lo], axis=2).astype(BF)
    dot_ = dctx.T.reshape(8, 64, 256)
    bias = jnp.where(tiles.T > 0, 0.0, -1e30).astype(F32)
    bias = jnp.repeat(bias, 128, axis=1)
    return bias, qt4, qs2, dot_


def front(pieces, slots, w_hi, w_lo, rows, span=512, unroll=32):
    width = 512
    n = len(pieces)
    count = sum(p.shape[0] for p in pieces)
    def kernel(*refs):
        idx = refs[0]
        parts = refs[1:1 + n]
        wh, wl, x_ref, kv_ref, table, flat, sem = refs[1 + n:]
        step = pl.program_id(0)
        @pl.when(step == 0)
        def _():
            copies = []
            at = 0
            for j, p in enumerate(parts):
                copies.append(pltpu.make_async_copy(p, table.at[pl.ds(at, p.shape[0])], sem.at[j]))
                at += p.shape[0]
            for c in copies:
                c.start()
            for c in copies:
                c.wait()
        def body(i, c):
            for u in range(unroll):
                e = i * unroll + u
                a = idx[0, step * span + e]
                b = idx[1, step * span + e]
                a = pl.multiple_of(a * 4, 4)
                b = pl.multiple_of(b * 4, 4)
                flat[pl.ds(pl.multiple_of(e * 4, 4), 4), :] = table[pl.ds(a, 4), :] + table[pl.ds(b, 4), :]
            return c
        lax.fori_loop(0, span // unroll, body, 0)
        x = jnp.concatenate([flat[pl.ds(j, span, stride=4), :] for j in range(4)], axis=1)
        x_ref[...] = x
        hi, lo = halves(x)
        kv_ref[...] = dot_nn(hi, wh[...]) + dot_nn(hi, wl[...]) + dot_nn(lo, wh[...])
    return pl.pallas_call(
        kernel,
        grid=(rows // span,),
        in_specs=[pl.BlockSpec(memory_space=pltpu.SMEM)]
        + [pl.BlockSpec(memory_space=pl.ANY)] * n
        + [pl.BlockSpec(w_hi.shape, lambda i: (0, 0))] * 2,
        out_specs=[pl.BlockSpec((span, width), lambda i: (i, 0)), pl.BlockSpec((span, 2 * width), lambda i: (i, 0))],
        out_shape=[jax.ShapeDtypeStruct((rows, width), F32), jax.ShapeDtypeStruct((rows, 2 * width), F32)],
        scratch_shapes=[pltpu.VMEM((count, 128), F32), pltpu.VMEM((span * 4, 128), F32), pltpu.SemaphoreType.DMA((n,))],
        compiler_params=pltpu.CompilerParams(vmem_limit_bytes=56 * MIB),
        cost_estimate=pl.CostEstimate(flops=40_000_000_000, bytes_accessed=32 * MIB, transcendentals=0),
    )(slots, *pieces, w_hi, w_lo)

def back(slots, own, dk, dv, wt_hi, wt_lo, qx, count, span=512, unroll=32, chains=4):
    rows, width = dk.shape
    def kernel(idx, own_ref, dk_ref, dv_ref, wh, wl, qx_ref, acc, *more):
        *others, dx, flat = more
        accs = [acc, *others]
        step = pl.program_id(0)
        @pl.when(step == 0)
        def _():
            def clear(i, c):
                at = pl.ds(pl.multiple_of(i * 512, 512), 512)
                for a in accs:
                    a[at, :] = jnp.zeros((512, 128), F32)
                return c
            lax.fori_loop(0, count * 4 // 512, clear, 0)
        khi, klo = halves(dk_ref[...])
        vhi, vlo = halves(dv_ref[...])
        hi = jnp.concatenate([khi, vhi], axis=1)
        lo = jnp.concatenate([klo, vlo], axis=1)
        dx[...] = dot_nn(hi, wh[...]) + dot_nn(hi, wl[...]) + dot_nn(lo, wh[...])
        @pl.when(own_ref[0] // 2 == step)
        def _():
            at = pl.ds(pl.multiple_of(own_ref[0] % 2 * 256, 256), 256)
            dx[at, :] += qx_ref[...]
        for j in range(4):
            flat[pl.ds(j, span, stride=4), :] = dx[:, j * 128:(j + 1) * 128]
        def body(i, c):
            for u in range(unroll):
                e = i * unroll + u
                a = pl.multiple_of(idx[0, step * span + e] * 4, 4)
                b = pl.multiple_of(idx[1, step * span + e] * 4, 4)
                row = flat[pl.ds(pl.multiple_of(e * 4, 4), 4), :]
                k = u % (chains // 2) * 2
                accs[k][pl.ds(a, 4), :] += row
                accs[k + 1][pl.ds(b, 4), :] += row
            return c
        lax.fori_loop(0, span // unroll, body, 0)
        @pl.when(step == rows // span - 1)
        def _():
            def add(i, c):
                at = pl.ds(pl.multiple_of(i * 512, 512), 512)
                acc[at, :] = sum(a[at, :] for a in accs)
                return c
            lax.fori_loop(0, count * 4 // 512, add, 0)
    return pl.pallas_call(
        kernel,
        grid=(rows // span,),
        in_specs=[pl.BlockSpec(memory_space=pltpu.SMEM)] * 2
        + [pl.BlockSpec((span, width), lambda i: (i, 0))] * 2
        + [pl.BlockSpec((2 * width, width), lambda i: (0, 0))] * 2
        + [pl.BlockSpec(qx.shape, lambda i: (0, 0))],
        out_specs=[pl.BlockSpec((count * 4, 128), lambda i: (0, 0), pipeline_mode=pl.Buffered(1))],
        out_shape=[jax.ShapeDtypeStruct((count * 4, 128), F32)],
        scratch_shapes=[pltpu.VMEM((count * 4, 128), F32)] * (chains - 1) + [pltpu.VMEM((span, width), F32), pltpu.VMEM((span * 4, 128), F32)],
        compiler_params=pltpu.CompilerParams(vmem_limit_bytes=56 * MIB),
        cost_estimate=pl.CostEstimate(flops=40_000_000_000, bytes_accessed=24 * MIB, transcendentals=0),
    )(slots, own, dk, dv, wt_hi, wt_lo, qx)[0]


def both_weights(dk, dv, x, span=512):
    rows, width = x.shape

    def kernel(dk_ref, dv_ref, x_ref, w_ref):
        @pl.when(pl.program_id(0) == 0)
        def _():
            w_ref[...] = jnp.zeros_like(w_ref)

        xhi, xlo = halves(x_ref[...])
        for j, ref in enumerate((dk_ref, dv_ref)):
            hi, lo = halves(ref[...])
            w_ref[:, j * width:(j + 1) * width] += dot_tn(xhi, hi) + dot_tn(xhi, lo) + dot_tn(xlo, hi)

    return pl.pallas_call(
        kernel,
        grid=(rows // span,),
        in_specs=[pl.BlockSpec((span, width), lambda i: (i, 0))] * 3,
        out_specs=pl.BlockSpec((width, 2 * width), lambda i: (0, 0)),
        out_shape=jax.ShapeDtypeStruct((width, 2 * width), F32),
        compiler_params=pltpu.CompilerParams(vmem_limit_bytes=56 * MIB),
        cost_estimate=pl.CostEstimate(flops=20_000_000_000, bytes_accessed=26 * MIB, transcendentals=0),
    )(dk, dv, x)


Z = ("zl", "zh")
SIZES = {"x": 4, "y": 4, Z: 4, "c": 2}


def place(axis, i):
    return i % 2 * 2 + i // 2 if axis == Z else i


def move(v, axis, to):
    n = SIZES[axis]
    return lax.ppermute(v, axis, [(place(axis, i), place(axis, to(i))) for i in range(n)])


def shift(v, axis, s):
    return move(v, axis, lambda i: (i + s) % SIZES[axis])


def ring_gather(v, axis):
    n = v.shape[0] // 2
    before = shift(v, axis, 1)
    after = shift(v, axis, -1)
    far_a = shift(before[:n], axis, 1)
    far_b = shift(after[n:], axis, -1)
    return [v, before, after, far_a, far_b]


def table_gather(shard):
    c = lax.axis_index("c")
    half = shard.shape[0] // 2
    mine = lax.dynamic_slice_in_dim(shard, c * half, half, 0)
    a1, a2 = mine[:half // 2], mine[half // 2:]
    q = half // 4
    za = shift(a2[:q], Z, 1)
    zb = shift(a2[q:], Z, -1)
    s1 = ring_gather(a1, "x")
    v2 = jnp.concatenate([a2, za, zb], 0)
    s2 = ring_gather(v2, "x")
    z1 = shift(jnp.concatenate(s1[:2], 0), Z, 1)
    z2 = shift(jnp.concatenate(s1[2:], 0), Z, -1)
    first = jnp.concatenate(s1 + [z1, z2], 0)
    other_first = shift(first, "c", 1)
    second = jnp.concatenate(s2, 0)
    other_second = shift(second, "c", 1)
    return first, second, other_first, other_second


SIDES = (lambda i: i ^ 1, lambda i: 3 - i)
GROUPS = (
    ((("x", 0), ("x", 1)), (("y", 0), ("y", 1), (Z, 0), (Z, 1))),
    ((("y", 0), ("y", 1)), ((Z, 0), (Z, 1), ("x", 0), ("x", 1))),
)


def side_bit(bit, at):
    axis, side = bit
    return (at[axis] + 1) // 2 % 2 if side == 0 else at[axis] // 2


def halve(v, dim, bit):
    keep = lax.index_in_dim(v, 0, dim, keepdims=False)
    send = lax.index_in_dim(v, 1, dim, keepdims=False)
    if bit == "c":
        return keep + shift(send, "c", 1)
    return keep + move(send, bit[0], SIDES[bit[1]])


def scatter_table(terms):
    out = []
    for v, (first, rest) in zip(terms.reshape(2, *[2] * 8, -1, 128), GROUPS):
        v = halve(v, 0, "c")
        a = halve(halve(v[0], 0, first[0]), 0, first[1])
        b = halve(halve(v[1], 0, first[1]), 0, first[0])
        w = jnp.stack([a, b])
        for bit in rest:
            w = halve(w, 1, bit)
        out.append(w)
    return jnp.stack(out).reshape(-1, 128)


def coordinates():
    zl, x, y, zh, c = (lax.axis_index(a) for a in ("zl", "x", "y", "zh", "c"))
    return {"x": x, "y": y, Z: zh * 2 + zl, "c": c, "zl": zl, "zh": zh}


def table_place(row, me):
    owner, local = row // 512, row % 512
    half, part, within = local // 256, local % 256 // 128, local % 128
    turn = (owner % 4 - me["x"]) % 4
    order = jnp.where(turn == 0, 0, jnp.where(turn == 3, 1, jnp.where(turn == 1, 2, 3)))
    other = (owner // 4 != me["zl"]).astype(jnp.int32)
    first = other * 512 + order * 128 + within
    second = 1024 + order * 256 + other * 128 + within
    return jnp.where(half != me["c"], 2048, 0) + jnp.where(part == 0, first, second)


def scatter_place(row, me):
    owner, local = row // 512, row % 512
    seq, within = local // 32, local % 32
    at = {"x": owner % 4, "y": seq // 4, Z: seq // 2 % 2 * 2 + owner // 4, "c": seq % 2}
    group, sub, inner = within // 16, within // 8 % 2, within % 8

    def chain(bits):
        out = 0
        for bit in bits:
            out = out * 2 + (side_bit(bit, at) ^ side_bit(bit, me))
        return out

    spots = []
    for first, rest in GROUPS:
        lead = jnp.where(sub == 0, chain(first), chain(first[::-1]))
        spots.append(lead * 16 + chain(rest))
    spot = jnp.where(group == 0, *spots)
    return (((group * 2 + (at["c"] ^ me["c"])) * 2 + sub) * 64 + spot) * 8 + inner


DP = ("zl", "x")
SEQ = ("y", "zh", "c")


def on_device(
    item_table,
    serve_lists,
    event_slots,
    session_tiles,
    w_query,
    w_key,
    w_value,
    w_out,
    grad_attended,
):
    me = coordinates()
    seq = lax.axis_index(SEQ)
    pieces = table_gather(item_table.reshape(-1, 128))
    lists = lax.all_to_all(serve_lists[0, :, 0, :], DP, split_axis=0, concat_axis=0, tiled=True)
    slots = event_slots[0]
    rows = slots // TILE * 512 + lists.reshape(-1)[slots]
    rows = lax.all_to_all(
        jnp.broadcast_to(rows.reshape(1, 4, 128), (16, 4, 128)), SEQ, split_axis=0, concat_axis=0, tiled=True
    )
    rows = rows.reshape(16, 2, 256).transpose(1, 0, 2).reshape(2, 4096)
    w_both = jnp.concatenate([w_key, w_value], axis=1)
    w_hi, w_lo = split_xla(w_both)
    w_hi, w_lo = w_hi.astype(BF), w_lo.astype(BF)
    history, both = front(pieces, table_place(rows, me), w_hi, w_lo, 4096)
    inputs = lax.dynamic_slice_in_dim(history, seq * 256, 256, 0)
    cotangent = grad_attended[0]
    scale = HEAD_DIM ** (-0.5)
    queries = product(inputs, w_query, EXACT) * scale
    grad_context = product(cotangent, w_out.T)
    context_t, grad_queries_t, grad_keys, grad_values = make(SPAN)(
        *operands(queries, grad_context, session_tiles[0]), both
    )
    context = context_t.T
    grad_queries = grad_queries_t.T * scale
    attended = product(context, w_out)
    grad_out_w = product(context_t, cotangent)
    grad_query_w = product(inputs.T, grad_queries)
    query_terms = product(grad_queries, w_query.T)
    grad_both_w = both_weights(grad_keys, grad_values, history)
    local_w = (grad_query_w, grad_both_w, grad_out_w)
    grad_keys, grad_values, local_w = lax.optimization_barrier((grad_keys, grad_values, local_w))
    sums = lax.psum(local_w, DP + SEQ)
    terms = back(
        scatter_place(rows, me), seq.reshape(1), grad_keys, grad_values, w_hi.T, w_lo.T, query_terms, 4096
    )
    grad_table = scatter_table(terms).reshape(32, 512)
    sums, grad_table = lax.optimization_barrier((sums, grad_table))
    grad_query_w, grad_both_w, grad_out_w = sums
    grad_key_w, grad_value_w = grad_both_w[:, :512], grad_both_w[:, 512:]
    return (attended[None], grad_query_w, grad_key_w, grad_value_w, grad_out_w, grad_table)


def solution(mesh):
    fine = Mesh(mesh.devices.reshape(2, 4, 4, 2, 2), ("zl", "x", "y", "zh", "c"))
    return jax.shard_map(
        on_device,
        mesh=fine,
        in_specs=(
            P(DP, None),
            P(DP, None, SEQ, None),
            P(DP, None, SEQ),
            P(DP, SEQ, None),
            P(),
            P(),
            P(),
            P(),
            P(DP, SEQ, None),
        ),
        out_specs=(P(DP, SEQ, None), P(), P(), P(), P(), P(DP + SEQ, None)),
        check_vma=False,
    )
```

```python
import jax
import jax.numpy as jnp
from jax import lax
from jax.experimental import pallas as pl
from jax.experimental.pallas import tpu as pltpu
from jax.sharding import Mesh, PartitionSpec as P

HEADS = 8
HEAD_DIM = 64
TILE = 128
SPAN = 1024
MIB = 1024 * 1024
BF = jnp.bfloat16
F32 = jnp.float32
EXACT = lax.Precision.HIGHEST
THREE = lax.Precision.HIGH


def product(left, right, precision=THREE):
    return jnp.dot(left, right, precision=precision, preferred_element_type=F32)

def dot_nn(a, b):
    return lax.dot_general(a, b, (((1,), (0,)), ((), ())), preferred_element_type=F32)

def dot_tn(a, b):
    return lax.dot_general(a, b, (((0,), (0,)), ((), ())), preferred_element_type=F32)

def halves(x):
    hi = x.astype(BF)
    lo = (x - hi.astype(F32)).astype(BF)
    return hi, lo

def make(span, un):
    def kernel(bias, qt4, qs2, dot_, k_ref, v_ref, ctx_ref, dq_ref, dk_ref, dv_ref, k2, v2, s_ref, ph, plo):
        rows = k_ref.shape[0]
        nb = rows // span
        tiles = span // 128
        low = lax.broadcasted_iota(jnp.int32, (span, 128), 1) < 64
        for head in range(2):
            def prepare(i, c):
                at = pl.ds(pl.multiple_of(i * span, span), span)
                for src, dst in ((k_ref, k2), (v_ref, v2)):
                    x = src[at, :]
                    hi = x.astype(BF).astype(F32)
                    lo = x - hi
                    if head == 0:
                        both = jnp.where(low, hi, pltpu.roll(lo, 64, 1))
                    else:
                        both = jnp.where(low, pltpu.roll(hi, 64, 1), lo)
                    dst[at, :] = both.astype(BF)
                return c
            lax.fori_loop(0, nb, prepare, 0)
            q4 = qt4[head]

            def score(i, peak):
                at = pl.ds(pl.multiple_of(i * span, span), span)
                k = k2[at, :]
                s = dot_nn(jnp.concatenate([k, k], axis=1), q4)
                parts = []
                for t in range(tiles):
                    st = s[t * 128:(t + 1) * 128] + bias[pl.ds(i * tiles + t, 1), :]
                    s_ref[pl.ds(pl.multiple_of(i * span + t * 128, 128), 128), :] = st
                    peak = jnp.maximum(peak, jnp.max(st.reshape(16, 8, 256), axis=0))
                return peak
            peak = lax.fori_loop(0, nb, score, jnp.full((8, 256), -3e38, F32), unroll=un)
            peak = jnp.max(peak, axis=0, keepdims=True)

            def weigh(i, carry):
                total, acc = carry
                at = pl.ds(pl.multiple_of(i * span, span), span)
                p = jnp.exp2(s_ref[at, :] - peak)
                total = total + jnp.sum(p.reshape(span // 8, 8, 256), axis=0)
                hi, lo = halves(p)
                ph[at, :] = hi
                plo[at, :] = lo
                v = v2[at, :]
                acc = acc + dot_tn(v, hi) + dot_tn(v, lo)
                return total, acc
            total, acc = lax.fori_loop(0, nb, weigh, (jnp.zeros((8, 256), F32), jnp.zeros((128, 256), F32)), unroll=un)
            share = 1.0 / jnp.sum(total, axis=0, keepdims=True)
            ctx = (acc[:64] + acc[64:]) * share
            ctx_ref[head * 64:(head + 1) * 64, :] = ctx
            g = dot_[head] * share
            delta = jnp.sum(g * ctx, axis=0, keepdims=True)
            ghi = g.astype(BF).astype(F32)
            glo = g - ghi
            g2 = jnp.concatenate([ghi, glo], axis=0)
            g4 = jnp.concatenate([ghi, ghi, glo, glo], axis=0).astype(BF)
            gn = g2.T.astype(BF)
            qn = qs2[head]

            def back(i, acc):
                at = pl.ds(pl.multiple_of(i * span, span), span)
                v = v2[at, :]
                k = k2[at, :]
                dp = dot_nn(jnp.concatenate([v, v], axis=1), g4)
                hi = ph[at, :]
                lo = plo[at, :]
                ds = (hi.astype(F32) + lo.astype(F32)) * (dp - delta)
                dv = dot_nn(hi, gn) + dot_nn(lo, gn)
                dv = dv + pltpu.roll(dv, 64, 1)
                shi, slo = halves(ds)
                dk = dot_nn(shi, qn) + dot_nn(slo, qn)
                dk = dk + pltpu.roll(dk, 64, 1)
                if head == 0:
                    dv_ref[at, :] = dv
                    dk_ref[at, :] = dk
                else:
                    dv_ref[at, :] = jnp.where(low, dv_ref[at, :], dv)
                    dk_ref[at, :] = jnp.where(low, dk_ref[at, :], dk)
                return acc + dot_tn(k, shi) + dot_tn(k, slo)
            acc = lax.fori_loop(0, nb, back, jnp.zeros((128, 256), F32), unroll=un)
            dq_ref[head * 64:(head + 1) * 64, :] = acc[:64] + acc[64:]

    def call(bias, qt4, qs2, dot_, kv):
        rows = kv.shape[0]
        pairs = 4
        return pl.pallas_call(
            kernel,
            grid=(pairs,),
            in_specs=[
                pl.BlockSpec(bias.shape, lambda p: (0, 0)),
                pl.BlockSpec((2, 256, 256), lambda p: (p, 0, 0)),
                pl.BlockSpec((2, 256, 128), lambda p: (p, 0, 0)),
                pl.BlockSpec((2, 64, 256), lambda p: (p, 0, 0)),
                pl.BlockSpec((rows, 128), lambda p: (0, p)),
                pl.BlockSpec((rows, 128), lambda p: (0, 4 + p)),
            ],
            out_specs=[
                pl.BlockSpec((128, 256), lambda p: (p, 0)),
                pl.BlockSpec((128, 256), lambda p: (p, 0)),
                pl.BlockSpec((rows, 128), lambda p: (0, p)),
                pl.BlockSpec((rows, 128), lambda p: (0, p)),
            ],
            out_shape=[
                jax.ShapeDtypeStruct((512, 256), F32),
                jax.ShapeDtypeStruct((512, 256), F32),
                jax.ShapeDtypeStruct((rows, 512), F32),
                jax.ShapeDtypeStruct((rows, 512), F32),
            ],
            scratch_shapes=[
                pltpu.VMEM((rows, 128), BF),
                pltpu.VMEM((rows, 128), BF),
                pltpu.VMEM((rows, 256), F32),
                pltpu.VMEM((rows, 256), BF),
                pltpu.VMEM((rows, 256), BF),
            ],
            compiler_params=pltpu.CompilerParams(vmem_limit_bytes=56 * MIB),
            cost_estimate=pl.CostEstimate(flops=90_000_000_000, bytes_accessed=32 * MIB, transcendentals=8 * MIB),
        )(bias, qt4, qs2, dot_, kv, kv)
    return call

def split_xla(x):
    hi = lax.reduce_precision(x, 8, 7)
    return hi, x - hi

def operands(q, dctx, tiles):
    log2e = 1.4426950408889634
    qt = (q * log2e).T.reshape(8, 64, 256)
    hi, lo = split_xla(qt)
    qt4 = jnp.concatenate([hi, hi, lo, lo], axis=1).astype(BF)
    qh = q.reshape(256, 8, 64).transpose(1, 0, 2)
    hi, lo = split_xla(qh)
    qs2 = jnp.concatenate([hi, lo], axis=2).astype(BF)
    dot_ = dctx.T.reshape(8, 64, 256)
    bias = jnp.where(tiles.T > 0, 0.0, -1e30).astype(F32)
    bias = jnp.repeat(bias, 128, axis=1)
    return bias, qt4, qs2, dot_


def front(pieces, slots, w_hi, w_lo, rows, span=512, unroll=32):
    width = 512
    n = len(pieces)
    count = sum(p.shape[0] for p in pieces)
    def kernel(*refs):
        idx = refs[0]
        parts = refs[1:1 + n]
        wh, wl, x_ref, kv_ref, table, flat, sem = refs[1 + n:]
        step = pl.program_id(0)
        @pl.when(step == 0)
        def _():
            copies = []
            at = 0
            for j, p in enumerate(parts):
                copies.append(pltpu.make_async_copy(p, table.at[pl.ds(at, p.shape[0])], sem.at[j]))
                at += p.shape[0]
            for c in copies:
                c.start()
            for c in copies:
                c.wait()
        def body(i, c):
            for u in range(unroll):
                e = i * unroll + u
                a = idx[0, step * span + e]
                b = idx[1, step * span + e]
                a = pl.multiple_of(a * 4, 4)
                b = pl.multiple_of(b * 4, 4)
                flat[pl.ds(pl.multiple_of(e * 4, 4), 4), :] = table[pl.ds(a, 4), :] + table[pl.ds(b, 4), :]
            return c
        lax.fori_loop(0, span // unroll, body, 0)
        x = jnp.concatenate([flat[pl.ds(j, span, stride=4), :] for j in range(4)], axis=1)
        x_ref[...] = x
        hi, lo = halves(x)
        kv_ref[...] = dot_nn(hi, wh[...]) + dot_nn(hi, wl[...]) + dot_nn(lo, wh[...])
    return pl.pallas_call(
        kernel,
        grid=(rows // span,),
        in_specs=[pl.BlockSpec(memory_space=pltpu.SMEM)]
        + [pl.BlockSpec(memory_space=pl.ANY)] * n
        + [pl.BlockSpec(w_hi.shape, lambda i: (0, 0))] * 2,
        out_specs=[pl.BlockSpec((span, width), lambda i: (i, 0)), pl.BlockSpec((span, 2 * width), lambda i: (i, 0))],
        out_shape=[jax.ShapeDtypeStruct((rows, width), F32), jax.ShapeDtypeStruct((rows, 2 * width), F32)],
        scratch_shapes=[pltpu.VMEM((count, 128), F32), pltpu.VMEM((span * 4, 128), F32), pltpu.SemaphoreType.DMA((n,))],
        compiler_params=pltpu.CompilerParams(vmem_limit_bytes=56 * MIB),
        cost_estimate=pl.CostEstimate(flops=40_000_000_000, bytes_accessed=32 * MIB, transcendentals=0),
    )(slots, *pieces, w_hi, w_lo)

def back(slots, own, dk, dv, wt_hi, wt_lo, qx, count, span=512, unroll=32, chains=4):
    rows, width = dk.shape
    def kernel(idx, own_ref, dk_ref, dv_ref, wh, wl, qx_ref, acc, *more):
        *others, dx, flat = more
        accs = [acc, *others]
        step = pl.program_id(0)
        @pl.when(step == 0)
        def _():
            def clear(i, c):
                at = pl.ds(pl.multiple_of(i * 512, 512), 512)
                for a in accs:
                    a[at, :] = jnp.zeros((512, 128), F32)
                return c
            lax.fori_loop(0, count * 4 // 512, clear, 0)
        khi, klo = halves(dk_ref[...])
        vhi, vlo = halves(dv_ref[...])
        hi = jnp.concatenate([khi, vhi], axis=1)
        lo = jnp.concatenate([klo, vlo], axis=1)
        dx[...] = dot_nn(hi, wh[...]) + dot_nn(hi, wl[...]) + dot_nn(lo, wh[...])
        @pl.when(own_ref[0] // 2 == step)
        def _():
            at = pl.ds(pl.multiple_of(own_ref[0] % 2 * 256, 256), 256)
            dx[at, :] += qx_ref[...]
        for j in range(4):
            flat[pl.ds(j, span, stride=4), :] = dx[:, j * 128:(j + 1) * 128]
        def body(i, c):
            for u in range(unroll):
                e = i * unroll + u
                a = pl.multiple_of(idx[0, step * span + e] * 4, 4)
                b = pl.multiple_of(idx[1, step * span + e] * 4, 4)
                row = flat[pl.ds(pl.multiple_of(e * 4, 4), 4), :]
                k = u % (chains // 2) * 2
                accs[k][pl.ds(a, 4), :] += row
                accs[k + 1][pl.ds(b, 4), :] += row
            return c
        lax.fori_loop(0, span // unroll, body, 0)
        @pl.when(step == rows // span - 1)
        def _():
            def add(i, c):
                at = pl.ds(pl.multiple_of(i * 512, 512), 512)
                acc[at, :] = sum(a[at, :] for a in accs)
                return c
            lax.fori_loop(0, count * 4 // 512, add, 0)
    return pl.pallas_call(
        kernel,
        grid=(rows // span,),
        in_specs=[pl.BlockSpec(memory_space=pltpu.SMEM)] * 2
        + [pl.BlockSpec((span, width), lambda i: (i, 0))] * 2
        + [pl.BlockSpec((2 * width, width), lambda i: (0, 0))] * 2
        + [pl.BlockSpec(qx.shape, lambda i: (0, 0))],
        out_specs=[pl.BlockSpec((count * 4, 128), lambda i: (0, 0), pipeline_mode=pl.Buffered(1))],
        out_shape=[jax.ShapeDtypeStruct((count * 4, 128), F32)],
        scratch_shapes=[pltpu.VMEM((count * 4, 128), F32)] * (chains - 1) + [pltpu.VMEM((span, width), F32), pltpu.VMEM((span * 4, 128), F32)],
        compiler_params=pltpu.CompilerParams(vmem_limit_bytes=56 * MIB),
        cost_estimate=pl.CostEstimate(flops=40_000_000_000, bytes_accessed=24 * MIB, transcendentals=0),
    )(slots, own, dk, dv, wt_hi, wt_lo, qx)[0]


def weight_blocks(places, dq_w, do_w, dk, dv, x, span=512):
    rows, width = x.shape
    steps = rows // span

    def kernel(at_ref, q_ref, o_ref, dk_ref, dv_ref, x_ref, out_ref, w_ref):
        @pl.when(pl.program_id(0) == 0)
        def _():
            w_ref[...] = jnp.zeros_like(w_ref)

        xhi, xlo = halves(x_ref[...])
        for j, ref in enumerate((dk_ref, dv_ref)):
            hi, lo = halves(ref[...])
            w_ref[:, j * width:(j + 1) * width] += dot_tn(xhi, hi) + dot_tn(xhi, lo) + dot_tn(xlo, hi)

        @pl.when(pl.program_id(0) == steps - 1)
        def _():
            def copy(i, c):
                cut = pl.ds(pl.multiple_of(i * 16, 16), 16)
                for j in range(16):
                    ref, k = ((w_ref, j), (q_ref, j - 8), (o_ref, j - 12))[(j >= 8) + (j >= 12)]
                    to = pl.ds(pl.multiple_of(at_ref[i * 16 + j] * 16, 16), 16)
                    out_ref[to, :] = ref[cut, k * 128:(k + 1) * 128]
                return c

            lax.fori_loop(0, 32, copy, 0)

    whole = pl.BlockSpec((width, width), lambda i: (0, 0))
    return pl.pallas_call(
        kernel,
        grid=(steps,),
        in_specs=[pl.BlockSpec(memory_space=pltpu.SMEM), whole, whole]
        + [pl.BlockSpec((span, width), lambda i: (i, 0))] * 3,
        out_specs=pl.BlockSpec((16 * width, 128), lambda i: (0, 0)),
        out_shape=jax.ShapeDtypeStruct((16 * width, 128), F32),
        scratch_shapes=[pltpu.VMEM((width, 2 * width), F32)],
        compiler_params=pltpu.CompilerParams(vmem_limit_bytes=56 * MIB),
        cost_estimate=pl.CostEstimate(flops=20_000_000_000, bytes_accessed=28 * MIB, transcendentals=0),
    )(places, dq_w, do_w, dk, dv, x)


def weights_of(places, pieces):
    width = 512
    n = len(pieces)

    def kernel(at_ref, *refs):
        parts, outs, all_ref, sem = refs[:n], refs[n:n + 4], refs[n + 4], refs[n + 5]
        copies, base = [], 0
        for j, p in enumerate(parts):
            copies.append(pltpu.make_async_copy(p, all_ref.at[pl.ds(base, p.shape[0])], sem.at[j]))
            base += p.shape[0]
        for c in copies:
            c.start()
        for c in copies:
            c.wait()

        def copy(i, c):
            cut = pl.ds(pl.multiple_of(i * 16, 16), 16)
            for j in range(16):
                k = j % 4
                at = pl.ds(pl.multiple_of(at_ref[i * 16 + j] * 16, 16), 16)
                outs[j // 4][cut, k * 128:(k + 1) * 128] = all_ref[at, :]
            return c

        lax.fori_loop(0, 32, copy, 0)

    return pl.pallas_call(
        kernel,
        in_specs=[pl.BlockSpec(memory_space=pltpu.SMEM)] + [pl.BlockSpec(memory_space=pl.ANY)] * n,
        out_specs=[pl.BlockSpec(memory_space=pltpu.VMEM)] * 4,
        out_shape=[jax.ShapeDtypeStruct((width, width), F32)] * 4,
        scratch_shapes=[pltpu.VMEM((16 * width, 128), F32), pltpu.SemaphoreType.DMA((n,))],
        compiler_params=pltpu.CompilerParams(vmem_limit_bytes=56 * MIB),
    )(places, *pieces)


Z = ("zl", "zh")
SIZES = {"x": 4, "y": 4, Z: 4, "c": 2}


def place(axis, i):
    return i % 2 * 2 + i // 2 if axis == Z else i


def move(v, axis, to):
    n = SIZES[axis]
    return lax.ppermute(v, axis, [(place(axis, i), place(axis, to(i))) for i in range(n)])


def shift(v, axis, s):
    return move(v, axis, lambda i: (i + s) % SIZES[axis])


def ring_gather(v, axis):
    n = v.shape[0] // 2
    before = shift(v, axis, 1)
    after = shift(v, axis, -1)
    far_a = shift(before[:n], axis, 1)
    far_b = shift(after[n:], axis, -1)
    return [v, before, after, far_a, far_b]


def table_gather(shard, extra):
    c = lax.axis_index("c")
    half = shard.shape[0] // 2
    mine = lax.dynamic_slice_in_dim(shard, c * half, half, 0)
    a1, a2 = mine[:half // 2], mine[half // 2:]
    q = half // 4
    za = shift(a2[:q], Z, 1)
    zb = shift(a2[q:], Z, -1)
    s1 = ring_gather(a1, "x")
    v2 = jnp.concatenate([a2, za, zb], 0)
    v2, extra = lax.optimization_barrier((v2, extra))
    s2 = ring_gather(v2, "x")
    z1 = shift(jnp.concatenate(s1[:2], 0), Z, 1)
    z2 = shift(jnp.concatenate(s1[2:], 0), Z, -1)
    first = jnp.concatenate(s1 + [z1, z2], 0)
    other_first = shift(first, "c", 1)
    second = jnp.concatenate(s2, 0)
    other_second = shift(second, "c", 1)
    return (first, second, other_first, other_second), extra


SIDES = (lambda i: i ^ 1, lambda i: 3 - i)
GROUPS = (
    ((("x", 0), ("x", 1)), (("y", 0), ("y", 1), (Z, 0), (Z, 1))),
    ((("y", 0), ("y", 1)), ((Z, 0), (Z, 1), ("x", 0), ("x", 1))),
)


def side_bit(bit, at):
    axis, side = bit
    return (at[axis] + 1) // 2 % 2 if side == 0 else at[axis] // 2


def across(v, bit):
    return move(v, bit[0], SIDES[bit[1]])


def halve(v, dim, bit):
    keep = lax.index_in_dim(v, 0, dim, keepdims=False)
    send = lax.index_in_dim(v, 1, dim, keepdims=False)
    return keep + across(send, bit)


def sum_over_devices(terms, blocks):
    bits = [2] * 6
    terms = terms.reshape(2, 2, 2, *bits, -1, 128)
    blocks = blocks.reshape(2, 2, 2, *bits, -1, 128)
    n = terms.shape[-2]
    mine, pieces = [], []
    for g, (first, rest) in enumerate(GROUPS):
        sent = shift(jnp.concatenate([terms[g, 1], blocks[g, 1]], axis=-2), "c", 1)
        v = jnp.concatenate([terms[g, 0], blocks[g, 0]], axis=-2) + sent
        a = halve(halve(v[0], 0, first[0]), 0, first[1])
        b = halve(halve(v[1], 0, first[1]), 0, first[0])
        w = jnp.stack([a, b])
        for bit in rest:
            w = halve(w, 1, bit)
        mine.append(w[:, :n])
        w = w[:, n:]
        for bit in rest[::-1]:
            w = jnp.stack([w, across(w, bit)], axis=1)
        a, b = w[0], w[1]
        for bit in first[::-1]:
            a = jnp.stack([a, across(a, bit)])
        for bit in first:
            b = jnp.stack([b, across(b, bit)])
        w = jnp.stack([a, b]).reshape(-1, 128)
        pieces += [w, shift(w, "c", 1)]
    return jnp.stack(mine).reshape(-1, 128), pieces


def coordinates():
    zl, x, y, zh, c = (lax.axis_index(a) for a in ("zl", "x", "y", "zh", "c"))
    return {"x": x, "y": y, Z: zh * 2 + zl, "c": c, "zl": zl, "zh": zh}


def table_place(row, me):
    owner, local = row // 512, row % 512
    half, part, within = local // 256, local % 256 // 128, local % 128
    turn = (owner % 4 - me["x"]) % 4
    order = jnp.where(turn == 0, 0, jnp.where(turn == 3, 1, jnp.where(turn == 1, 2, 3)))
    other = (owner // 4 != me["zl"]).astype(jnp.int32)
    first = other * 512 + order * 128 + within
    second = 1024 + order * 256 + other * 128 + within
    return jnp.where(half != me["c"], 2048, 0) + jnp.where(part == 0, first, second)


def scatter_place(row, me):
    owner, local = row // 512, row % 512
    seq, within = local // 32, local % 32
    at = {"x": owner % 4, "y": seq // 4, Z: seq // 2 % 2 * 2 + owner // 4, "c": seq % 2}
    group, sub, inner = within // 16, within // 8 % 2, within % 8

    def chain(bits):
        out = 0
        for bit in bits:
            out = out * 2 + (side_bit(bit, at) ^ side_bit(bit, me))
        return out

    spots = []
    for first, rest in GROUPS:
        lead = jnp.where(sub == 0, chain(first), chain(first[::-1]))
        spots.append(lead * 16 + chain(rest))
    spot = jnp.where(group == 0, *spots)
    return (((group * 2 + (at["c"] ^ me["c"])) * 2 + sub) * 64 + spot) * 8 + inner


def block_place(me):
    ids = jnp.arange(512, dtype=jnp.int32)
    group, sub = ids // 256, ids // 64 % 2

    def chain(bits):
        out = 0
        for bit in bits:
            out = out * 2 + side_bit(bit, me)
        return out

    spots = []
    for first, rest in GROUPS:
        lead = jnp.where(sub == 0, chain(first), chain(first[::-1]))
        spots.append(lead * 16 + chain(rest))
    return ids ^ (jnp.where(group == 0, *spots) + me["c"] * 128)


DP = ("zl", "x")
SEQ = ("y", "zh", "c")


def on_device(
    item_table,
    serve_lists,
    event_slots,
    session_tiles,
    w_query,
    w_key,
    w_value,
    w_out,
    grad_attended,
):
    me = coordinates()
    seq = lax.axis_index(SEQ)
    lists = lax.all_to_all(serve_lists[0, :, 0, :], DP, split_axis=0, concat_axis=0, tiled=True)
    slots = event_slots[0]
    rows = slots // TILE * 512 + lists.reshape(-1)[slots]
    rows = lax.all_to_all(
        jnp.broadcast_to(rows.reshape(1, 4, 128), (16, 4, 128)), SEQ, split_axis=0, concat_axis=0, tiled=True
    )
    pieces, rows = table_gather(item_table.reshape(-1, 128), rows)
    rows = rows.reshape(16, 2, 256).transpose(1, 0, 2).reshape(2, 4096)
    w_both = jnp.concatenate([w_key, w_value], axis=1)
    w_hi, w_lo = split_xla(w_both)
    w_hi, w_lo = w_hi.astype(BF), w_lo.astype(BF)
    history, both = front(pieces, table_place(rows, me), w_hi, w_lo, 4096)
    inputs = lax.dynamic_slice_in_dim(history, seq * 256, 256, 0)
    cotangent = grad_attended[0]
    scale = HEAD_DIM ** (-0.5)
    queries = product(inputs, w_query, EXACT) * scale
    grad_context = product(cotangent, w_out.T)
    context_t, grad_queries_t, grad_keys, grad_values = make(SPAN, 2)(
        *operands(queries, grad_context, session_tiles[0]), both
    )
    context = context_t.T
    grad_queries = grad_queries_t.T * scale
    attended = product(context, w_out)
    grad_out_w = product(context_t, cotangent)
    grad_query_w = product(inputs.T, grad_queries)
    query_terms = product(grad_queries, w_query.T)
    places = block_place(me)
    blocks = weight_blocks(places, grad_query_w, grad_out_w, grad_keys, grad_values, history)
    terms = back(
        scatter_place(rows, me), seq.reshape(1), grad_keys, grad_values, w_hi.T, w_lo.T, query_terms, 4096
    )
    grad_table, pieces = sum_over_devices(terms, blocks)
    grad_key_w, grad_value_w, grad_query_w, grad_out_w = weights_of(places, pieces)
    grad_table = grad_table.reshape(32, 512)
    return (attended[None], grad_query_w, grad_key_w, grad_value_w, grad_out_w, grad_table)


def solution(mesh):
    fine = Mesh(mesh.devices.reshape(2, 4, 4, 2, 2), ("zl", "x", "y", "zh", "c"))
    return jax.shard_map(
        on_device,
        mesh=fine,
        in_specs=(
            P(DP, None),
            P(DP, None, SEQ, None),
            P(DP, None, SEQ),
            P(DP, SEQ, None),
            P(),
            P(),
            P(),
            P(),
            P(DP, SEQ, None),
        ),
        out_specs=(P(DP, SEQ, None), P(), P(), P(), P(), P(DP + SEQ, None)),
        check_vma=False,
    )
```

```python
import jax
import jax.numpy as jnp
from jax import lax
from jax.experimental import pallas as pl
from jax.experimental.pallas import tpu as pltpu
from jax.sharding import Mesh, PartitionSpec as P

HEADS = 8
HEAD_DIM = 64
TILE = 128
SPAN = 1024
MIB = 1024 * 1024
BF = jnp.bfloat16
F32 = jnp.float32
EXACT = lax.Precision.HIGHEST
THREE = lax.Precision.HIGH
NEGATIVE = -1e30
LOG2E = 1.4426950408889634


def product(left, right, precision=THREE):
    return jnp.dot(left, right, precision=precision, preferred_element_type=F32)

def dot_nn(a, b):
    return lax.dot_general(a, b, (((1,), (0,)), ((), ())), preferred_element_type=F32)

def dot_tn(a, b):
    return lax.dot_general(a, b, (((0,), (0,)), ((), ())), preferred_element_type=F32)

def halves(x):
    hi = x.astype(BF)
    lo = (x - hi.astype(F32)).astype(BF)
    return hi, lo

def make(span, un):
    def kernel(bias, q_ref, g_ref, k_ref, v_ref, ctx_ref, dq_ref, dk_ref, dv_ref, k2, v2, s_ref, ph, plo):
        rows = k_ref.shape[0]
        nb = rows // span
        tiles = span // 128
        low = lax.broadcasted_iota(jnp.int32, (span, 128), 1) < 64
        q, near = q_ref[...], lax.broadcasted_iota(jnp.int32, (256, 128), 1) < 64
        q_hi = q.astype(BF).astype(F32)
        q_lo = q - q_hi
        qt = (q * LOG2E).T
        contexts, slopes = [], []
        gt = g_ref[...].T
        for head in range(2):
            def prepare(i, c):
                at = pl.ds(pl.multiple_of(i * span, span), span)
                for src, dst in ((k_ref, k2), (v_ref, v2)):
                    x = src[at, :]
                    hi = x.astype(BF).astype(F32)
                    lo = x - hi
                    if head == 0:
                        both = jnp.where(low, hi, pltpu.roll(lo, 64, 1))
                    else:
                        both = jnp.where(low, pltpu.roll(hi, 64, 1), lo)
                    dst[at, :] = both.astype(BF)
                return c
            lax.fori_loop(0, nb, prepare, 0)
            top = qt[head * 64:(head + 1) * 64]
            top_hi = top.astype(BF).astype(F32)
            top_lo = top - top_hi
            q4 = jnp.concatenate([top_hi, top_hi, top_lo, top_lo], axis=0).astype(BF)
            if head == 0:
                qn = jnp.where(near, q_hi, pltpu.roll(q_lo, 64, 1)).astype(BF)
            else:
                qn = jnp.where(near, pltpu.roll(q_hi, 64, 1), q_lo).astype(BF)

            def score(i, peak):
                at = pl.ds(pl.multiple_of(i * span, span), span)
                k = k2[at, :]
                s = dot_nn(jnp.concatenate([k, k], axis=1), q4)
                parts = []
                for t in range(tiles):
                    st = s[t * 128:(t + 1) * 128] + bias[pl.ds(i * tiles + t, 1), :]
                    s_ref[pl.ds(pl.multiple_of(i * span + t * 128, 128), 128), :] = st
                    peak = jnp.maximum(peak, jnp.max(st.reshape(16, 8, 256), axis=0))
                return peak
            peak = lax.fori_loop(0, nb, score, jnp.full((8, 256), -3e38, F32), unroll=un)
            peak = jnp.max(peak, axis=0, keepdims=True)

            def weigh(i, carry):
                total, acc = carry
                at = pl.ds(pl.multiple_of(i * span, span), span)
                p = jnp.exp2(s_ref[at, :] - peak)
                total = total + jnp.sum(p.reshape(span // 8, 8, 256), axis=0)
                hi, lo = halves(p)
                ph[at, :] = hi
                plo[at, :] = lo
                v = v2[at, :]
                acc = acc + dot_tn(v, hi) + dot_tn(v, lo)
                return total, acc
            total, acc = lax.fori_loop(0, nb, weigh, (jnp.zeros((8, 256), F32), jnp.zeros((128, 256), F32)), unroll=un)
            share = 1.0 / jnp.sum(total, axis=0, keepdims=True)
            ctx = (acc[:64] + acc[64:]) * share
            contexts.append(ctx)
            g = gt[head * 64:(head + 1) * 64] * share
            delta = jnp.sum(g * ctx, axis=0, keepdims=True)
            ghi = g.astype(BF).astype(F32)
            glo = g - ghi
            g2 = jnp.concatenate([ghi, glo], axis=0)
            g4 = jnp.concatenate([ghi, ghi, glo, glo], axis=0).astype(BF)
            gn = g2.T.astype(BF)

            def back(i, acc):
                at = pl.ds(pl.multiple_of(i * span, span), span)
                v = v2[at, :]
                k = k2[at, :]
                dp = dot_nn(jnp.concatenate([v, v], axis=1), g4)
                hi = ph[at, :]
                lo = plo[at, :]
                ds = (hi.astype(F32) + lo.astype(F32)) * (dp - delta)
                dv = dot_nn(hi, gn) + dot_nn(lo, gn)
                dv = dv + pltpu.roll(dv, 64, 1)
                shi, slo = halves(ds)
                dk = dot_nn(shi, qn) + dot_nn(slo, qn)
                dk = dk + pltpu.roll(dk, 64, 1)
                if head == 0:
                    dv_ref[at, :] = dv
                    dk_ref[at, :] = dk
                else:
                    dv_ref[at, :] = jnp.where(low, dv_ref[at, :], dv)
                    dk_ref[at, :] = jnp.where(low, dk_ref[at, :], dk)
                return acc + dot_tn(k, shi) + dot_tn(k, slo)
            acc = lax.fori_loop(0, nb, back, jnp.zeros((128, 256), F32), unroll=un)
            slopes.append(acc[:64] + acc[64:])
        ctx_ref[...] = jnp.concatenate(contexts, axis=0).T
        dq_ref[...] = jnp.concatenate(slopes, axis=0).T * 0.125

    def call(bias, q, g, kv):
        rows = kv.shape[0]
        pairs = 4
        return pl.pallas_call(
            kernel,
            grid=(pairs,),
            in_specs=[
                pl.BlockSpec(bias.shape, lambda p: (0, 0)),
                pl.BlockSpec((256, 128), lambda p: (0, p)),
                pl.BlockSpec((256, 128), lambda p: (0, p)),
                pl.BlockSpec((rows, 128), lambda p: (0, p)),
                pl.BlockSpec((rows, 128), lambda p: (0, 4 + p)),
            ],
            out_specs=[
                pl.BlockSpec((256, 128), lambda p: (0, p)),
                pl.BlockSpec((256, 128), lambda p: (0, p)),
                pl.BlockSpec((rows, 128), lambda p: (0, p)),
                pl.BlockSpec((rows, 128), lambda p: (0, p)),
            ],
            out_shape=[
                jax.ShapeDtypeStruct((256, 512), F32),
                jax.ShapeDtypeStruct((256, 512), F32),
                jax.ShapeDtypeStruct((rows, 512), F32),
                jax.ShapeDtypeStruct((rows, 512), F32),
            ],
            scratch_shapes=[
                pltpu.VMEM((rows, 128), BF),
                pltpu.VMEM((rows, 128), BF),
                pltpu.VMEM((rows, 256), F32),
                pltpu.VMEM((rows, 256), BF),
                pltpu.VMEM((rows, 256), BF),
            ],
            compiler_params=pltpu.CompilerParams(vmem_limit_bytes=56 * MIB),
            cost_estimate=pl.CostEstimate(flops=90_000_000_000, bytes_accessed=32 * MIB, transcendentals=8 * MIB),
        )(bias, q, g, kv, kv)
    return call

def tile_bias(tiles):
    return jnp.repeat(jnp.where(tiles.T > 0, 0.0, NEGATIVE).astype(F32), TILE, axis=1)


def front(pieces, slots, w_key, w_value, rows, span=512):
    width, n = 512, len(pieces)
    steps = rows // span
    part = 32
    count = sum(p.shape[0] for p in pieces)

    def kernel(idx, *refs):
        parts = refs[:n]
        wk, wv, x_ref, kv_ref, table, flat, wh, wl, sem = refs[n:]
        step = pl.program_id(0)

        @pl.when(step == 0)
        def _():
            copies, at = [], 0
            for j, p in enumerate(parts):
                copies.append(pltpu.make_async_copy(p, table.at[pl.ds(at, p.shape[0])], sem.at[j]))
                at += p.shape[0]
            for c in copies:
                c.start()
            for j, w in enumerate((wk, wv)):
                hi, lo = halves(w[...])
                wh[:, j * width:(j + 1) * width] = hi
                wl[:, j * width:(j + 1) * width] = lo
            for c in copies:
                c.wait()

        base = step * span

        def body(j, c):
            for u in range(part):
                e = j * part + u
                a = pl.multiple_of(idx[0, base + e] * 4, 4)
                b = pl.multiple_of(idx[1, base + e] * 4, 4)
                flat[pl.ds(pl.multiple_of(e * 4, 4), 4), :] = table[pl.ds(a, 4), :] + table[pl.ds(b, 4), :]
            return c

        lax.fori_loop(0, span // part, body, 0)
        x = jnp.concatenate([flat[pl.ds(j, span, stride=4), :] for j in range(4)], axis=1)
        x_ref[...] = x
        hi, lo = halves(x)
        kv_ref[...] = dot_nn(hi, wh[...]) + dot_nn(hi, wl[...]) + dot_nn(lo, wh[...])

    whole = pl.BlockSpec((width, width), lambda i: (0, 0))
    return pl.pallas_call(
        kernel,
        grid=(steps,),
        in_specs=[pl.BlockSpec(memory_space=pltpu.SMEM)] + [pl.BlockSpec(memory_space=pl.ANY)] * n + [whole] * 2,
        out_specs=[
            pl.BlockSpec((span, width), lambda i: (i, 0)),
            pl.BlockSpec((span, 2 * width), lambda i: (i, 0)),
        ],
        out_shape=[jax.ShapeDtypeStruct((rows, width), F32), jax.ShapeDtypeStruct((rows, 2 * width), F32)],
        scratch_shapes=[
            pltpu.VMEM((count, 128), F32),
            pltpu.VMEM((span * 4, 128), F32),
            pltpu.VMEM((width, 2 * width), BF),
            pltpu.VMEM((width, 2 * width), BF),
            pltpu.SemaphoreType.DMA((n,)),
        ],
        compiler_params=pltpu.CompilerParams(vmem_limit_bytes=56 * MIB),
        cost_estimate=pl.CostEstimate(flops=40_000_000_000, bytes_accessed=32 * MIB, transcendentals=0),
    )(slots, *pieces, w_key, w_value)


def back(slots, own, dk, dv, w_key, w_value, qx, count, span=512):
    rows, width = dk.shape
    steps = rows // span
    part = 32
    quarter = count

    def kernel(idx, own_ref, dk_ref, dv_ref, wk, wv, qx_ref, *refs):
        outs, accs = refs[:4], refs[4:8]
        dx, flat, wh, wl, sem = refs[8:]
        step = pl.program_id(0)

        @pl.when(step == 0)
        def _():
            def clear(i, c):
                at = pl.ds(pl.multiple_of(i * 512, 512), 512)
                for a in accs:
                    a[at, :] = jnp.zeros((512, 128), F32)
                return c

            lax.fori_loop(0, count * 4 // 512, clear, 0)
            for j, w in enumerate((wk, wv)):
                hi, lo = halves(w[...].T)
                wh[j * width:(j + 1) * width, :] = hi
                wl[j * width:(j + 1) * width, :] = lo

        khi, klo = halves(dk_ref[...])
        vhi, vlo = halves(dv_ref[...])
        hi = jnp.concatenate([khi, vhi], axis=1)
        lo = jnp.concatenate([klo, vlo], axis=1)
        dx[...] = dot_nn(hi, wh[...]) + dot_nn(hi, wl[...]) + dot_nn(lo, wh[...])

        @pl.when(own_ref[0] // 2 == step)
        def _():
            at = pl.ds(pl.multiple_of(own_ref[0] % 2 * 256, 256), 256)
            dx[at, :] += qx_ref[...]

        for j in range(4):
            flat[pl.ds(j, span, stride=4), :] = dx[:, j * 128:(j + 1) * 128]
        base = step * span

        def body(j, c):
            for u in range(part):
                e = j * part + u
                a = pl.multiple_of(idx[0, base + e] * 4, 4)
                b = pl.multiple_of(idx[1, base + e] * 4, 4)
                row = flat[pl.ds(pl.multiple_of(e * 4, 4), 4), :]
                k = u % 2 * 2
                accs[k][pl.ds(a, 4), :] += row
                accs[k + 1][pl.ds(b, 4), :] += row
            return c

        lax.fori_loop(0, span // part, body, 0)

        @pl.when(step == steps - 1)
        def _():
            copies = []
            for q in range(4):
                def add(i, c):
                    at = pl.ds(pl.multiple_of(q * quarter + i * 512, 512), 512)
                    accs[0][at, :] = (accs[0][at, :] + accs[1][at, :]) + (accs[2][at, :] + accs[3][at, :])
                    return c

                lax.fori_loop(0, quarter // 512, add, 0)
                copies.append(pltpu.make_async_copy(accs[0].at[pl.ds(q * quarter, quarter)], outs[q], sem.at[q]))
                copies[-1].start()
            for c in copies:
                c.wait()

    whole = pl.BlockSpec((width, width), lambda i: (0, 0))
    return pl.pallas_call(
        kernel,
        grid=(steps,),
        in_specs=[pl.BlockSpec(memory_space=pltpu.SMEM)] * 2
        + [pl.BlockSpec((span, width), lambda i: (i, 0))] * 2
        + [whole] * 2
        + [pl.BlockSpec(qx.shape, lambda i: (0, 0))],
        out_specs=[pl.BlockSpec(memory_space=pl.ANY)] * 4,
        out_shape=[jax.ShapeDtypeStruct((quarter, 128), F32)] * 4,
        scratch_shapes=[pltpu.VMEM((count * 4, 128), F32)] * 4
        + [
            pltpu.VMEM((span, width), F32),
            pltpu.VMEM((span * 4, 128), F32),
            pltpu.VMEM((2 * width, width), BF),
            pltpu.VMEM((2 * width, width), BF),
            pltpu.SemaphoreType.DMA((4,)),
        ],
        compiler_params=pltpu.CompilerParams(vmem_limit_bytes=58 * MIB),
        cost_estimate=pl.CostEstimate(flops=40_000_000_000, bytes_accessed=24 * MIB, transcendentals=0),
    )(slots, own, dk, dv, w_key, w_value, qx)


def weight_blocks(places, dq_w, do_w, dk, dv, x, span=512):
    rows, width = x.shape
    steps = rows // span

    def kernel(at_ref, q_ref, o_ref, dk_ref, dv_ref, x_ref, *refs):
        outs, out_ref, w_ref, sem = refs[:4], *refs[4:]
        @pl.when(pl.program_id(0) == 0)
        def _():
            w_ref[...] = jnp.zeros_like(w_ref)

        xhi, xlo = halves(x_ref[...])
        for j, ref in enumerate((dk_ref, dv_ref)):
            hi, lo = halves(ref[...])
            w_ref[:, j * width:(j + 1) * width] += dot_tn(xhi, hi) + dot_tn(xhi, lo) + dot_tn(xlo, hi)

        @pl.when(pl.program_id(0) == steps - 1)
        def _():
            def copy(i, c):
                cut = pl.ds(pl.multiple_of(i * 16, 16), 16)
                for j in range(16):
                    ref, k = ((w_ref, j), (q_ref, j - 8), (o_ref, j - 12))[(j >= 8) + (j >= 12)]
                    to = pl.ds(pl.multiple_of(at_ref[i * 16 + j] * 16, 16), 16)
                    out_ref[to, :] = ref[cut, k * 128:(k + 1) * 128]
                return c

            lax.fori_loop(0, 32, copy, 0)
            copies = [pltpu.make_async_copy(out_ref.at[pl.ds(j * 4 * width, 4 * width)], outs[j], sem.at[j]) for j in range(4)]
            for c in copies:
                c.start()
            for c in copies:
                c.wait()

    whole = pl.BlockSpec((width, width), lambda i: (0, 0))
    return pl.pallas_call(
        kernel,
        grid=(steps,),
        in_specs=[pl.BlockSpec(memory_space=pltpu.SMEM), whole, whole]
        + [pl.BlockSpec((span, width), lambda i: (i, 0))] * 3,
        out_specs=[pl.BlockSpec(memory_space=pl.ANY)] * 4,
        out_shape=[jax.ShapeDtypeStruct((4 * width, 128), F32)] * 4,
        scratch_shapes=[
            pltpu.VMEM((16 * width, 128), F32),
            pltpu.VMEM((width, 2 * width), F32),
            pltpu.SemaphoreType.DMA((4,)),
        ],
        compiler_params=pltpu.CompilerParams(vmem_limit_bytes=56 * MIB),
        cost_estimate=pl.CostEstimate(flops=20_000_000_000, bytes_accessed=28 * MIB, transcendentals=0),
    )(places, dq_w, do_w, dk, dv, x)


def weights_of(places, pieces):
    width = 512
    n = len(pieces)

    def kernel(at_ref, *refs):
        parts, outs, all_ref, sem = refs[:n], refs[n:n + 4], refs[n + 4], refs[n + 5]
        copies, base = [], 0
        for j, p in enumerate(parts):
            copies.append(pltpu.make_async_copy(p, all_ref.at[pl.ds(base, p.shape[0])], sem.at[j]))
            base += p.shape[0]
        for c in copies:
            c.start()
        for c in copies:
            c.wait()

        def copy(i, c):
            cut = pl.ds(pl.multiple_of(i * 16, 16), 16)
            for j in range(16):
                k = j % 4
                at = pl.ds(pl.multiple_of(at_ref[i * 16 + j] * 16, 16), 16)
                outs[j // 4][cut, k * 128:(k + 1) * 128] = all_ref[at, :]
            return c

        lax.fori_loop(0, 32, copy, 0)

    return pl.pallas_call(
        kernel,
        in_specs=[pl.BlockSpec(memory_space=pltpu.SMEM)] + [pl.BlockSpec(memory_space=pl.ANY)] * n,
        out_specs=[pl.BlockSpec(memory_space=pltpu.VMEM)] * 4,
        out_shape=[jax.ShapeDtypeStruct((width, width), F32)] * 4,
        scratch_shapes=[pltpu.VMEM((16 * width, 128), F32), pltpu.SemaphoreType.DMA((n,))],
        compiler_params=pltpu.CompilerParams(vmem_limit_bytes=56 * MIB),
    )(places, *pieces)


Z = ("zl", "zh")
SIZES = {"x": 4, "y": 4, Z: 4, "c": 2}


def place(axis, i):
    return i % 2 * 2 + i // 2 if axis == Z else i


def move(v, axis, to):
    n = SIZES[axis]
    return lax.ppermute(v, axis, [(place(axis, i), place(axis, to(i))) for i in range(n)])


def shift(v, axis, s):
    return move(v, axis, lambda i: (i + s) % SIZES[axis])


def further(v, before, after, axis):
    n = v.shape[0] // 2
    return [v, before, after, shift(before[:n], axis, 1), shift(after[n:], axis, -1)]


def table_gather(shard, lists, rows_of):
    c = lax.axis_index("c")
    half = shard.shape[0] // 2
    mine = lax.dynamic_slice_in_dim(shard, c * half, half, 0)
    a1, a2 = mine[:half // 2], mine[half // 2:]
    before, after = shift(a1, "x", 1), shift(a1, "x", -1)
    q = half // 4
    za, zb = shift(a2[:q], Z, 1), shift(a2[q:], Z, -1)
    v2 = jnp.concatenate([a2, za, zb], 0)
    v2, before, after, lists = lax.optimization_barrier((v2, before, after, lists))
    s1 = further(a1, before, after, "x")
    before2, after2 = shift(v2, "x", 1), shift(v2, "x", -1)
    rows = rows_of(lists)
    up, down = jnp.concatenate(s1[:2], 0), jnp.concatenate(s1[2:], 0)
    up, down, rows = lax.optimization_barrier((up, down, rows))
    z1, z2 = shift(up, Z, 1), shift(down, Z, -1)
    s2 = further(v2, before2, after2, "x")
    second = jnp.concatenate(s2, 0)
    other_second = shift(second, "c", 1)
    first = jnp.concatenate([up, down, z1, z2], 0)
    other_first = shift(first, "c", 1)
    return (first, second, other_first, other_second), rows


SIDES = (lambda i: i ^ 1, lambda i: 3 - i)
GROUPS = (
    ((("x", 0), ("x", 1)), (("y", 0), ("y", 1), (Z, 0), (Z, 1))),
    ((("y", 0), ("y", 1)), ((Z, 0), (Z, 1), ("x", 0), ("x", 1))),
)


def side_bit(bit, at):
    axis, side = bit
    return (at[axis] + 1) // 2 % 2 if side == 0 else at[axis] // 2


def across(v, bit):
    return move(v, bit[0], SIDES[bit[1]])


def halve(v, dim, bit):
    keep = lax.index_in_dim(v, 0, dim, keepdims=False)
    send = lax.index_in_dim(v, 1, dim, keepdims=False)
    return keep + across(send, bit)


def sum_over_devices(terms, blocks):
    bits = [2] * 6
    terms = [v.reshape(2, *bits, -1, 128) for v in terms]
    blocks = [v.reshape(2, *bits, -1, 128) for v in blocks]
    n = terms[0].shape[-2]
    mine, pieces = [], []
    for g, (first, rest) in enumerate(GROUPS):
        sent = shift(jnp.concatenate([terms[2 * g + 1], blocks[2 * g + 1]], axis=-2), "c", 1)
        v = jnp.concatenate([terms[2 * g], blocks[2 * g]], axis=-2) + sent
        a = halve(halve(v[0], 0, first[0]), 0, first[1])
        b = halve(halve(v[1], 0, first[1]), 0, first[0])
        w = jnp.stack([a, b])
        for bit in rest:
            w = halve(w, 1, bit)
        mine.append(w[:, :n])
        w = w[:, n:]
        for bit in rest[::-1]:
            w = jnp.stack([w, across(w, bit)], axis=1)
        a, b = w[0], w[1]
        for bit in first[::-1]:
            a = jnp.stack([a, across(a, bit)])
        for bit in first:
            b = jnp.stack([b, across(b, bit)])
        w = jnp.stack([a, b]).reshape(-1, 128)
        pieces += [w, shift(w, "c", 1)]
    return jnp.stack(mine).reshape(-1, 128), pieces


def coordinates():
    zl, x, y, zh, c = (lax.axis_index(a) for a in ("zl", "x", "y", "zh", "c"))
    return {"x": x, "y": y, Z: zh * 2 + zl, "c": c, "zl": zl, "zh": zh}


def table_place(row, me):
    owner, local = row // 512, row % 512
    half, part, within = local // 256, local % 256 // 128, local % 128
    turn = (owner % 4 - me["x"]) % 4
    order = jnp.where(turn == 0, 0, jnp.where(turn == 3, 1, jnp.where(turn == 1, 2, 3)))
    other = (owner // 4 != me["zl"]).astype(jnp.int32)
    first = other * 512 + order * 128 + within
    second = 1024 + order * 256 + other * 128 + within
    return jnp.where(half != me["c"], 2048, 0) + jnp.where(part == 0, first, second)


def scatter_place(row, me):
    owner, local = row // 512, row % 512
    seq, within = local // 32, local % 32
    at = {"x": owner % 4, "y": seq // 4, Z: seq // 2 % 2 * 2 + owner // 4, "c": seq % 2}
    group, sub, inner = within // 16, within // 8 % 2, within % 8

    def chain(bits):
        out = 0
        for bit in bits:
            out = out * 2 + (side_bit(bit, at) ^ side_bit(bit, me))
        return out

    spots = []
    for first, rest in GROUPS:
        lead = jnp.where(sub == 0, chain(first), chain(first[::-1]))
        spots.append(lead * 16 + chain(rest))
    spot = jnp.where(group == 0, *spots)
    return (((group * 2 + (at["c"] ^ me["c"])) * 2 + sub) * 64 + spot) * 8 + inner


def block_place(me):
    ids = jnp.arange(512, dtype=jnp.int32)
    group, sub = ids // 256, ids // 64 % 2

    def chain(bits):
        out = 0
        for bit in bits:
            out = out * 2 + side_bit(bit, me)
        return out

    spots = []
    for first, rest in GROUPS:
        lead = jnp.where(sub == 0, chain(first), chain(first[::-1]))
        spots.append(lead * 16 + chain(rest))
    return ids ^ (jnp.where(group == 0, *spots) + me["c"] * 128)


DP = ("zl", "x")
SEQ = ("y", "zh", "c")


def on_device(
    item_table,
    serve_lists,
    event_slots,
    session_tiles,
    w_query,
    w_key,
    w_value,
    w_out,
    grad_attended,
):
    me = coordinates()
    seq = lax.axis_index(SEQ)
    slots = event_slots[0]

    def rows_of(lists):
        rows = slots // TILE * 512 + lists.reshape(-1)[slots]
        rows = jnp.broadcast_to(rows.reshape(1, 4, 128), (16, 4, 128))
        return lax.all_to_all(rows, SEQ, split_axis=0, concat_axis=0, tiled=True)

    lists = lax.all_to_all(serve_lists[0, :, 0, :], DP, split_axis=0, concat_axis=0, tiled=True)
    pieces, rows = table_gather(item_table.reshape(-1, 128), lists, rows_of)
    rows = rows.reshape(16, 2, 256).transpose(1, 0, 2).reshape(2, 4096)
    history, both = front(pieces, table_place(rows, me), w_key, w_value, 4096)
    inputs = lax.dynamic_slice_in_dim(history, seq * 256, 256, 0)
    cotangent = grad_attended[0]
    scale = HEAD_DIM ** (-0.5)
    queries = product(inputs, w_query, EXACT) * scale
    grad_context = product(cotangent, w_out.T)
    context, grad_queries, grad_keys, grad_values = make(SPAN, 2)(
        tile_bias(session_tiles[0]), queries, grad_context, both
    )
    attended = product(context, w_out)
    grad_out_w = product(context.T, cotangent)
    grad_query_w = product(inputs.T, grad_queries)
    query_terms = product(grad_queries, w_query.T)
    places = block_place(me)
    blocks = weight_blocks(places, grad_query_w, grad_out_w, grad_keys, grad_values, history)
    terms = back(
        scatter_place(rows, me), seq.reshape(1), grad_keys, grad_values, w_key, w_value, query_terms, 4096
    )
    grad_table, pieces = sum_over_devices(terms, blocks)
    grad_key_w, grad_value_w, grad_query_w, grad_out_w = weights_of(places, pieces)
    grad_table = grad_table.reshape(32, 512)
    return (attended[None], grad_query_w, grad_key_w, grad_value_w, grad_out_w, grad_table)


def solution(mesh):
    fine = Mesh(mesh.devices.reshape(2, 4, 4, 2, 2), ("zl", "x", "y", "zh", "c"))
    return jax.shard_map(
        on_device,
        mesh=fine,
        in_specs=(
            P(DP, None),
            P(DP, None, SEQ, None),
            P(DP, None, SEQ),
            P(DP, SEQ, None),
            P(),
            P(),
            P(),
            P(),
            P(DP, SEQ, None),
        ),
        out_specs=(P(DP, SEQ, None), P(), P(), P(), P(), P(DP + SEQ, None)),
        check_vma=False,
    )
```

```python
import jax
import jax.numpy as jnp
from jax import lax
from jax.experimental import pallas as pl
from jax.experimental.pallas import tpu as pltpu
from jax.sharding import Mesh, PartitionSpec as P

HEADS = 8
HEAD_DIM = 64
TILE = 128
SPAN = 1024
MIB = 1024 * 1024
BF = jnp.bfloat16
F32 = jnp.float32
EXACT = lax.Precision.HIGHEST
THREE = lax.Precision.HIGH
NEGATIVE = -1e30
LOG2E = 1.4426950408889634


def product(left, right, precision=THREE):
    return jnp.dot(left, right, precision=precision, preferred_element_type=F32)

def dot_nn(a, b):
    return lax.dot_general(a, b, (((1,), (0,)), ((), ())), preferred_element_type=F32)

def dot_tn(a, b):
    return lax.dot_general(a, b, (((0,), (0,)), ((), ())), preferred_element_type=F32)

def halves(x):
    hi = x.astype(BF)
    lo = (x - hi.astype(F32)).astype(BF)
    return hi, lo

def make(span, un):
    def kernel(bias, q_ref, g_ref, k_ref, v_ref, ctx_ref, dq_ref, dk_ref, dv_ref, k2, v2, s_ref, ph, plo):
        rows = k_ref.shape[0]
        nb = rows // span
        tiles = span // 128
        low = lax.broadcasted_iota(jnp.int32, (span, 128), 1) < 64
        q, near = q_ref[...], lax.broadcasted_iota(jnp.int32, (256, 128), 1) < 64
        q_hi = q.astype(BF).astype(F32)
        q_lo = q - q_hi
        qt = (q * LOG2E).T
        contexts, slopes = [], []
        gt = g_ref[...].T
        for head in range(2):
            def prepare(i, c):
                at = pl.ds(pl.multiple_of(i * span, span), span)
                for src, dst in ((k_ref, k2), (v_ref, v2)):
                    x = src[at, :]
                    hi = x.astype(BF).astype(F32)
                    lo = x - hi
                    if head == 0:
                        both = jnp.where(low, hi, pltpu.roll(lo, 64, 1))
                    else:
                        both = jnp.where(low, pltpu.roll(hi, 64, 1), lo)
                    dst[at, :] = both.astype(BF)
                return c
            lax.fori_loop(0, nb, prepare, 0)
            top = qt[head * 64:(head + 1) * 64]
            top_hi = top.astype(BF).astype(F32)
            top_lo = top - top_hi
            q4 = jnp.concatenate([top_hi, top_hi, top_lo, top_lo], axis=0).astype(BF)
            if head == 0:
                qn = jnp.where(near, q_hi, pltpu.roll(q_lo, 64, 1)).astype(BF)
            else:
                qn = jnp.where(near, pltpu.roll(q_hi, 64, 1), q_lo).astype(BF)

            def score(i, peak):
                at = pl.ds(pl.multiple_of(i * span, span), span)
                k = k2[at, :]
                s = dot_nn(jnp.concatenate([k, k], axis=1), q4)
                parts = []
                for t in range(tiles):
                    st = s[t * 128:(t + 1) * 128] + bias[pl.ds(i * tiles + t, 1), :]
                    s_ref[pl.ds(pl.multiple_of(i * span + t * 128, 128), 128), :] = st
                    peak = jnp.maximum(peak, jnp.max(st.reshape(16, 8, 256), axis=0))
                return peak
            peak = lax.fori_loop(0, nb, score, jnp.full((8, 256), -3e38, F32), unroll=un)
            peak = jnp.max(peak, axis=0, keepdims=True)

            def weigh(i, carry):
                total, acc = carry
                at = pl.ds(pl.multiple_of(i * span, span), span)
                p = jnp.exp2(s_ref[at, :] - peak)
                total = total + jnp.sum(p.reshape(span // 8, 8, 256), axis=0)
                hi, lo = halves(p)
                ph[at, :] = hi
                plo[at, :] = lo
                v = v2[at, :]
                acc = acc + dot_tn(v, hi) + dot_tn(v, lo)
                return total, acc
            total, acc = lax.fori_loop(0, nb, weigh, (jnp.zeros((8, 256), F32), jnp.zeros((128, 256), F32)), unroll=un)
            share = 1.0 / jnp.sum(total, axis=0, keepdims=True)
            ctx = (acc[:64] + acc[64:]) * share
            contexts.append(ctx)
            g = gt[head * 64:(head + 1) * 64] * share
            delta = jnp.sum(g * ctx, axis=0, keepdims=True)
            ghi = g.astype(BF).astype(F32)
            glo = g - ghi
            g2 = jnp.concatenate([ghi, glo], axis=0)
            g4 = jnp.concatenate([ghi, ghi, glo, glo], axis=0).astype(BF)
            gn = g2.T.astype(BF)

            def back(i, acc):
                at = pl.ds(pl.multiple_of(i * span, span), span)
                v = v2[at, :]
                k = k2[at, :]
                dp = dot_nn(jnp.concatenate([v, v], axis=1), g4)
                hi = ph[at, :]
                lo = plo[at, :]
                ds = (hi.astype(F32) + lo.astype(F32)) * (dp - delta)
                dv = dot_nn(hi, gn) + dot_nn(lo, gn)
                dv = dv + pltpu.roll(dv, 64, 1)
                shi, slo = halves(ds)
                dk = dot_nn(shi, qn) + dot_nn(slo, qn)
                dk = dk + pltpu.roll(dk, 64, 1)
                if head == 0:
                    dv_ref[at, :] = dv
                    dk_ref[at, :] = dk
                else:
                    dv_ref[at, :] = jnp.where(low, dv_ref[at, :], dv)
                    dk_ref[at, :] = jnp.where(low, dk_ref[at, :], dk)
                return acc + dot_tn(k, shi) + dot_tn(k, slo)
            acc = lax.fori_loop(0, nb, back, jnp.zeros((128, 256), F32), unroll=un)
            slopes.append(acc[:64] + acc[64:])
        ctx_ref[...] = jnp.concatenate(contexts, axis=0).T
        dq_ref[...] = jnp.concatenate(slopes, axis=0).T * 0.125

    def call(bias, q, g, kv):
        rows = kv.shape[0]
        pairs = 4
        return pl.pallas_call(
            kernel,
            grid=(pairs,),
            in_specs=[
                pl.BlockSpec(bias.shape, lambda p: (0, 0)),
                pl.BlockSpec((256, 128), lambda p: (0, p)),
                pl.BlockSpec((256, 128), lambda p: (0, p)),
                pl.BlockSpec((rows, 128), lambda p: (0, p)),
                pl.BlockSpec((rows, 128), lambda p: (0, 4 + p)),
            ],
            out_specs=[
                pl.BlockSpec((256, 128), lambda p: (0, p)),
                pl.BlockSpec((256, 128), lambda p: (0, p)),
                pl.BlockSpec((rows, 128), lambda p: (0, p)),
                pl.BlockSpec((rows, 128), lambda p: (0, p)),
            ],
            out_shape=[
                jax.ShapeDtypeStruct((256, 512), F32),
                jax.ShapeDtypeStruct((256, 512), F32),
                jax.ShapeDtypeStruct((rows, 512), F32),
                jax.ShapeDtypeStruct((rows, 512), F32),
            ],
            scratch_shapes=[
                pltpu.VMEM((rows, 128), BF),
                pltpu.VMEM((rows, 128), BF),
                pltpu.VMEM((rows, 256), F32),
                pltpu.VMEM((rows, 256), BF),
                pltpu.VMEM((rows, 256), BF),
            ],
            compiler_params=pltpu.CompilerParams(vmem_limit_bytes=56 * MIB),
            cost_estimate=pl.CostEstimate(flops=90_000_000_000, bytes_accessed=32 * MIB, transcendentals=8 * MIB),
        )(bias, q, g, kv, kv)
    return call

def tile_bias(tiles):
    return jnp.repeat(jnp.where(tiles.T > 0, 0.0, NEGATIVE).astype(F32), TILE, axis=1)


def front(pieces, slots, w_key, w_value, rows, span=512):
    width, n = 512, len(pieces)
    steps = rows // span
    part = 32
    count = sum(p.shape[0] for p in pieces)

    def kernel(idx, *refs):
        parts = refs[:n]
        wk, wv, x_ref, kv_ref, table, flat, wh, wl, sem = refs[n:]
        step = pl.program_id(0)

        @pl.when(step == 0)
        def _():
            copies, at = [], 0
            for j, p in enumerate(parts):
                copies.append(pltpu.make_async_copy(p, table.at[pl.ds(at, p.shape[0])], sem.at[j]))
                at += p.shape[0]
            for c in copies:
                c.start()
            for j, w in enumerate((wk, wv)):
                hi, lo = halves(w[...])
                wh[:, j * width:(j + 1) * width] = hi
                wl[:, j * width:(j + 1) * width] = lo
            for c in copies:
                c.wait()

        base = step * span

        def body(j, c):
            for u in range(part):
                e = j * part + u
                a = pl.multiple_of(idx[base + e], 4)
                b = pl.multiple_of(idx[rows + base + e], 4)
                flat[pl.ds(pl.multiple_of(e * 4, 4), 4), :] = table[pl.ds(a, 4), :] + table[pl.ds(b, 4), :]
            return c

        lax.fori_loop(0, span // part, body, 0)
        x = jnp.concatenate([flat[pl.ds(j, span, stride=4), :] for j in range(4)], axis=1)
        x_ref[...] = x
        hi, lo = halves(x)
        kv_ref[...] = dot_nn(hi, wh[...]) + dot_nn(hi, wl[...]) + dot_nn(lo, wh[...])

    whole = pl.BlockSpec((width, width), lambda i: (0, 0))
    return pl.pallas_call(
        kernel,
        grid=(steps,),
        in_specs=[pl.BlockSpec(memory_space=pltpu.SMEM)] + [pl.BlockSpec(memory_space=pl.ANY)] * n + [whole] * 2,
        out_specs=[
            pl.BlockSpec((span, width), lambda i: (i, 0)),
            pl.BlockSpec((span, 2 * width), lambda i: (i, 0)),
        ],
        out_shape=[jax.ShapeDtypeStruct((rows, width), F32), jax.ShapeDtypeStruct((rows, 2 * width), F32)],
        scratch_shapes=[
            pltpu.VMEM((count, 128), F32),
            pltpu.VMEM((span * 4, 128), F32),
            pltpu.VMEM((width, 2 * width), BF),
            pltpu.VMEM((width, 2 * width), BF),
            pltpu.SemaphoreType.DMA((n,)),
        ],
        compiler_params=pltpu.CompilerParams(vmem_limit_bytes=56 * MIB),
        cost_estimate=pl.CostEstimate(flops=40_000_000_000, bytes_accessed=32 * MIB, transcendentals=0),
    )(slots, *pieces, w_key, w_value)


def back(slots, own, dk, dv, w_key, w_value, qx, count, span=512):
    rows, width = dk.shape
    steps = rows // span
    part = 32
    quarter = count

    def kernel(idx, own_ref, dk_ref, dv_ref, wk, wv, qx_ref, *refs):
        outs, accs = refs[:4], refs[4:8]
        dx, flat, wh, wl, sem = refs[8:]
        step = pl.program_id(0)

        @pl.when(step == 0)
        def _():
            def clear(i, c):
                at = pl.ds(pl.multiple_of(i * 512, 512), 512)
                for a in accs:
                    a[at, :] = jnp.zeros((512, 128), F32)
                return c

            lax.fori_loop(0, count * 4 // 512, clear, 0)
            for j, w in enumerate((wk, wv)):
                hi, lo = halves(w[...].T)
                wh[j * width:(j + 1) * width, :] = hi
                wl[j * width:(j + 1) * width, :] = lo

        khi, klo = halves(dk_ref[...])
        vhi, vlo = halves(dv_ref[...])
        hi = jnp.concatenate([khi, vhi], axis=1)
        lo = jnp.concatenate([klo, vlo], axis=1)
        dx[...] = dot_nn(hi, wh[...]) + dot_nn(hi, wl[...]) + dot_nn(lo, wh[...])

        @pl.when(own_ref[0] // 2 == step)
        def _():
            at = pl.ds(pl.multiple_of(own_ref[0] % 2 * 256, 256), 256)
            dx[at, :] += qx_ref[...]

        for j in range(4):
            flat[pl.ds(j, span, stride=4), :] = dx[:, j * 128:(j + 1) * 128]
        base = step * span

        def body(j, c):
            for u in range(part):
                e = j * part + u
                a = pl.multiple_of(idx[base + e], 4)
                b = pl.multiple_of(idx[rows + base + e], 4)
                row = flat[pl.ds(pl.multiple_of(e * 4, 4), 4), :]
                k = u % 2 * 2
                accs[k][pl.ds(a, 4), :] += row
                accs[k + 1][pl.ds(b, 4), :] += row
            return c

        lax.fori_loop(0, span // part, body, 0)

        @pl.when(step == steps - 1)
        def _():
            copies = []
            for q in range(4):
                def add(i, c):
                    at = pl.ds(pl.multiple_of(q * quarter + i * 512, 512), 512)
                    accs[0][at, :] = (accs[0][at, :] + accs[1][at, :]) + (accs[2][at, :] + accs[3][at, :])
                    return c

                lax.fori_loop(0, quarter // 512, add, 0)
                copies.append(pltpu.make_async_copy(accs[0].at[pl.ds(q * quarter, quarter)], outs[q], sem.at[q]))
                copies[-1].start()
            for c in copies:
                c.wait()

    whole = pl.BlockSpec((width, width), lambda i: (0, 0))
    return pl.pallas_call(
        kernel,
        grid=(steps,),
        in_specs=[pl.BlockSpec(memory_space=pltpu.SMEM)] * 2
        + [pl.BlockSpec((span, width), lambda i: (i, 0))] * 2
        + [whole] * 2
        + [pl.BlockSpec(qx.shape, lambda i: (0, 0))],
        out_specs=[pl.BlockSpec(memory_space=pl.ANY)] * 4,
        out_shape=[jax.ShapeDtypeStruct((quarter, 128), F32)] * 4,
        scratch_shapes=[pltpu.VMEM((count * 4, 128), F32)] * 4
        + [
            pltpu.VMEM((span, width), F32),
            pltpu.VMEM((span * 4, 128), F32),
            pltpu.VMEM((2 * width, width), BF),
            pltpu.VMEM((2 * width, width), BF),
            pltpu.SemaphoreType.DMA((4,)),
        ],
        compiler_params=pltpu.CompilerParams(vmem_limit_bytes=58 * MIB),
        cost_estimate=pl.CostEstimate(flops=40_000_000_000, bytes_accessed=24 * MIB, transcendentals=0),
    )(slots, own, dk, dv, w_key, w_value, qx)


def weight_blocks(places, dq_w, do_w, dk, dv, x, span=512):
    rows, width = x.shape
    steps = rows // span

    def kernel(at_ref, q_ref, o_ref, dk_ref, dv_ref, x_ref, *refs):
        outs, out_ref, w_ref, sem = refs[:4], *refs[4:]
        @pl.when(pl.program_id(0) == 0)
        def _():
            w_ref[...] = jnp.zeros_like(w_ref)

        xhi, xlo = halves(x_ref[...])
        for j, ref in enumerate((dk_ref, dv_ref)):
            hi, lo = halves(ref[...])
            w_ref[:, j * width:(j + 1) * width] += dot_tn(xhi, hi) + dot_tn(xhi, lo) + dot_tn(xlo, hi)

        @pl.when(pl.program_id(0) == steps - 1)
        def _():
            def copy(i, c):
                cut = pl.ds(pl.multiple_of(i * 16, 16), 16)
                for j in range(16):
                    ref, k = ((w_ref, j), (q_ref, j - 8), (o_ref, j - 12))[(j >= 8) + (j >= 12)]
                    to = pl.ds(pl.multiple_of(at_ref[i * 16 + j] * 16, 16), 16)
                    out_ref[to, :] = ref[cut, k * 128:(k + 1) * 128]
                return c

            lax.fori_loop(0, 32, copy, 0)
            copies = [pltpu.make_async_copy(out_ref.at[pl.ds(j * 4 * width, 4 * width)], outs[j], sem.at[j]) for j in range(4)]
            for c in copies:
                c.start()
            for c in copies:
                c.wait()

    whole = pl.BlockSpec((width, width), lambda i: (0, 0))
    return pl.pallas_call(
        kernel,
        grid=(steps,),
        in_specs=[pl.BlockSpec(memory_space=pltpu.SMEM), whole, whole]
        + [pl.BlockSpec((span, width), lambda i: (i, 0))] * 3,
        out_specs=[pl.BlockSpec(memory_space=pl.ANY)] * 4,
        out_shape=[jax.ShapeDtypeStruct((4 * width, 128), F32)] * 4,
        scratch_shapes=[
            pltpu.VMEM((16 * width, 128), F32),
            pltpu.VMEM((width, 2 * width), F32),
            pltpu.SemaphoreType.DMA((4,)),
        ],
        compiler_params=pltpu.CompilerParams(vmem_limit_bytes=56 * MIB),
        cost_estimate=pl.CostEstimate(flops=20_000_000_000, bytes_accessed=28 * MIB, transcendentals=0),
    )(places, dq_w, do_w, dk, dv, x)


def weights_of(places, pieces):
    width = 512
    n = len(pieces)

    def kernel(at_ref, *refs):
        parts, outs, all_ref, sem = refs[:n], refs[n:n + 4], refs[n + 4], refs[n + 5]
        copies, base = [], 0
        for j, p in enumerate(parts):
            copies.append(pltpu.make_async_copy(p, all_ref.at[pl.ds(base, p.shape[0])], sem.at[j]))
            base += p.shape[0]
        for c in copies:
            c.start()
        for c in copies:
            c.wait()

        def copy(i, c):
            cut = pl.ds(pl.multiple_of(i * 16, 16), 16)
            for j in range(16):
                k = j % 4
                at = pl.ds(pl.multiple_of(at_ref[i * 16 + j] * 16, 16), 16)
                outs[j // 4][cut, k * 128:(k + 1) * 128] = all_ref[at, :]
            return c

        lax.fori_loop(0, 32, copy, 0)

    return pl.pallas_call(
        kernel,
        in_specs=[pl.BlockSpec(memory_space=pltpu.SMEM)] + [pl.BlockSpec(memory_space=pl.ANY)] * n,
        out_specs=[pl.BlockSpec(memory_space=pltpu.VMEM)] * 4,
        out_shape=[jax.ShapeDtypeStruct((width, width), F32)] * 4,
        scratch_shapes=[pltpu.VMEM((16 * width, 128), F32), pltpu.SemaphoreType.DMA((n,))],
        compiler_params=pltpu.CompilerParams(vmem_limit_bytes=56 * MIB),
    )(places, *pieces)


Z = ("zl", "zh")
SIZES = {"x": 4, "y": 4, Z: 4, "c": 2}


def place(axis, i):
    return i % 2 * 2 + i // 2 if axis == Z else i


def move(v, axis, to):
    n = SIZES[axis]
    return lax.ppermute(v, axis, [(place(axis, i), place(axis, to(i))) for i in range(n)])


def shift(v, axis, s):
    return move(v, axis, lambda i: (i + s) % SIZES[axis])


def further(v, before, after, axis):
    n = v.shape[0] // 2
    return [v, before, after, shift(before[:n], axis, 1), shift(after[n:], axis, -1)]


def table_gather(shard, lists, rows_of, places_of, extra):
    c = lax.axis_index("c")
    half = shard.shape[0] // 2
    mine = lax.dynamic_slice_in_dim(shard, c * half, half, 0)
    a1, a2 = mine[:half // 2], mine[half // 2:]
    before, after = shift(a1, "x", 1), shift(a1, "x", -1)
    q = half // 4
    za, zb = shift(a2[:q], Z, 1), shift(a2[q:], Z, -1)
    v2 = jnp.concatenate([a2, za, zb], 0)
    v2, before, after, lists = lax.optimization_barrier((v2, before, after, lists))
    s1 = further(a1, before, after, "x")
    before2, after2 = shift(v2, "x", 1), shift(v2, "x", -1)
    rows = rows_of(lists)
    up, down = jnp.concatenate(s1[:2], 0), jnp.concatenate(s1[2:], 0)
    z1, z2 = shift(up, Z, 1), shift(down, Z, -1)
    before2, after2, rows = lax.optimization_barrier((before2, after2, rows))
    s2 = further(v2, before2, after2, "x")
    second = jnp.concatenate(s2, 0)
    second, places, extra = lax.optimization_barrier((second, places_of(rows), extra))
    other_second = shift(second, "c", 1)
    first = jnp.concatenate([up, down, z1, z2], 0)
    other_first = shift(first, "c", 1)
    return (first, second, other_first, other_second), places, extra


SIDES = (lambda i: i ^ 1, lambda i: 3 - i)
GROUPS = (
    ((("x", 0), ("x", 1)), (("y", 0), ("y", 1), (Z, 0), (Z, 1))),
    ((("y", 0), ("y", 1)), ((Z, 0), (Z, 1), ("x", 0), ("x", 1))),
)


def side_bit(bit, at):
    axis, side = bit
    return (at[axis] + 1) // 2 % 2 if side == 0 else at[axis] // 2


def across(v, bit):
    return move(v, bit[0], SIDES[bit[1]])


def halve(v, dim, bit):
    keep = lax.index_in_dim(v, 0, dim, keepdims=False)
    send = lax.index_in_dim(v, 1, dim, keepdims=False)
    return keep + across(send, bit)


def sum_over_devices(terms, blocks, extra):
    bits = [2] * 6
    terms = [v.reshape(2, *bits, -1, 128) for v in terms]
    blocks = [v.reshape(2, *bits, -1, 128) for v in blocks]
    n = terms[0].shape[-2]
    mine, pieces = [], []
    for g, (first, rest) in enumerate(GROUPS):
        sent = shift(jnp.concatenate([terms[2 * g + 1], blocks[2 * g + 1]], axis=-2), "c", 1)
        v = jnp.concatenate([terms[2 * g], blocks[2 * g]], axis=-2) + sent
        a = halve(halve(v[0], 0, first[0]), 0, first[1])
        b = halve(v[1], 0, first[1])
        if g == 0:
            b, extra = lax.optimization_barrier((b, extra))
        b = halve(b, 0, first[0])
        w = jnp.stack([a, b])
        for bit in rest:
            w = halve(w, 1, bit)
        mine.append(w[:, :n])
        w = w[:, n:]
        for bit in rest[::-1]:
            w = jnp.stack([w, across(w, bit)], axis=1)
        a, b = w[0], w[1]
        for bit in first[::-1]:
            a = jnp.stack([a, across(a, bit)])
        for bit in first:
            b = jnp.stack([b, across(b, bit)])
        w = jnp.stack([a, b]).reshape(-1, 128)
        pieces += [w, shift(w, "c", 1)]
    return jnp.stack(mine).reshape(-1, 128), pieces, extra


def coordinates():
    zl, x, y, zh, c = (lax.axis_index(a) for a in ("zl", "x", "y", "zh", "c"))
    return {"x": x, "y": y, Z: zh * 2 + zl, "c": c, "zl": zl, "zh": zh}


def table_place(row, me):
    owner, local = row // 512, row % 512
    half, part, within = local // 256, local % 256 // 128, local % 128
    turn = (owner % 4 - me["x"]) % 4
    order = jnp.where(turn == 0, 0, jnp.where(turn == 3, 1, jnp.where(turn == 1, 2, 3)))
    other = (owner // 4 != me["zl"]).astype(jnp.int32)
    first = other * 512 + order * 128 + within
    second = 1024 + order * 256 + other * 128 + within
    return jnp.where(half != me["c"], 2048, 0) + jnp.where(part == 0, first, second)


def scatter_place(row, me):
    owner, local = row // 512, row % 512
    seq, within = local // 32, local % 32
    at = {"x": owner % 4, "y": seq // 4, Z: seq // 2 % 2 * 2 + owner // 4, "c": seq % 2}
    group, sub, inner = within // 16, within // 8 % 2, within % 8

    def chain(bits):
        out = 0
        for bit in bits:
            out = out * 2 + (side_bit(bit, at) ^ side_bit(bit, me))
        return out

    spots = []
    for first, rest in GROUPS:
        lead = jnp.where(sub == 0, chain(first), chain(first[::-1]))
        spots.append(lead * 16 + chain(rest))
    spot = jnp.where(group == 0, *spots)
    return (((group * 2 + (at["c"] ^ me["c"])) * 2 + sub) * 64 + spot) * 8 + inner


def block_place(me):
    ids = jnp.arange(512, dtype=jnp.int32)
    group, sub = ids // 256, ids // 64 % 2

    def chain(bits):
        out = 0
        for bit in bits:
            out = out * 2 + side_bit(bit, me)
        return out

    spots = []
    for first, rest in GROUPS:
        lead = jnp.where(sub == 0, chain(first), chain(first[::-1]))
        spots.append(lead * 16 + chain(rest))
    return ids ^ (jnp.where(group == 0, *spots) + me["c"] * 128)


DP = ("zl", "x")
SEQ = ("y", "zh", "c")


def on_device(
    item_table,
    serve_lists,
    event_slots,
    session_tiles,
    w_query,
    w_key,
    w_value,
    w_out,
    grad_attended,
):
    me = coordinates()
    seq = lax.axis_index(SEQ)
    slots = event_slots[0]

    def rows_of(lists):
        rows = slots // TILE * 512 + lists.reshape(-1)[slots]
        rows = jnp.broadcast_to(rows.reshape(1, 4, 128), (16, 4, 128))
        return lax.all_to_all(rows, SEQ, split_axis=0, concat_axis=0, tiled=True)

    def places_of(rows):
        rows = rows.reshape(16, 2, 256).transpose(1, 0, 2).reshape(2, 4096)
        return [(place(rows, me) * 4).reshape(-1) for place in (table_place, scatter_place)]

    cotangent = grad_attended[0]
    lists = lax.all_to_all(serve_lists[0, :, 0, :], DP, split_axis=0, concat_axis=0, tiled=True)
    pieces, (from_places, to_places), (grad_context, bias) = table_gather(
        item_table.reshape(-1, 128),
        lists,
        rows_of,
        places_of,
        (product(cotangent, w_out.T), tile_bias(session_tiles[0])),
    )
    history, both = front(pieces, from_places, w_key, w_value, 4096)
    inputs = lax.dynamic_slice_in_dim(history, seq * 256, 256, 0)
    scale = HEAD_DIM ** (-0.5)
    queries = product(inputs, w_query, EXACT) * scale
    context, grad_queries, grad_keys, grad_values = make(SPAN, 2)(
        bias, queries, grad_context, both
    )
    attended = product(context, w_out)
    grad_out_w = product(context.T, cotangent)
    grad_query_w = product(inputs.T, grad_queries)
    query_terms = product(grad_queries, w_query.T)
    places = block_place(me)
    blocks = weight_blocks(places, grad_query_w, grad_out_w, grad_keys, grad_values, history)
    terms = back(
        to_places, seq.reshape(1), grad_keys, grad_values, w_key, w_value, query_terms, 4096
    )
    grad_table, pieces, attended = sum_over_devices(terms, blocks, attended)
    grad_key_w, grad_value_w, grad_query_w, grad_out_w = weights_of(places, pieces)
    grad_table = grad_table.reshape(32, 512)
    return (attended[None], grad_query_w, grad_key_w, grad_value_w, grad_out_w, grad_table)


def solution(mesh):
    fine = Mesh(mesh.devices.reshape(2, 4, 4, 2, 2), ("zl", "x", "y", "zh", "c"))
    return jax.shard_map(
        on_device,
        mesh=fine,
        in_specs=(
            P(DP, None),
            P(DP, None, SEQ, None),
            P(DP, None, SEQ),
            P(DP, SEQ, None),
            P(),
            P(),
            P(),
            P(),
            P(DP, SEQ, None),
        ),
        out_specs=(P(DP, SEQ, None), P(), P(), P(), P(), P(DP + SEQ, None)),
        check_vma=False,
    )
```

```python
import jax
import jax.numpy as jnp
from jax import lax
from jax.experimental import pallas as pl
from jax.experimental.pallas import tpu as pltpu
from jax.sharding import Mesh, PartitionSpec as P

HEADS = 8
HEAD_DIM = 64
TILE = 128
SPAN = 1024
MIB = 1024 * 1024
BF = jnp.bfloat16
F32 = jnp.float32
EXACT = lax.Precision.HIGHEST
THREE = lax.Precision.HIGH
NEGATIVE = -1e30
LOG2E = 1.4426950408889634


def product(left, right, precision=THREE):
    return jnp.dot(left, right, precision=precision, preferred_element_type=F32)

def dot_nn(a, b):
    return lax.dot_general(a, b, (((1,), (0,)), ((), ())), preferred_element_type=F32)

def dot_tn(a, b):
    return lax.dot_general(a, b, (((0,), (0,)), ((), ())), preferred_element_type=F32)

def halves(x):
    hi = x.astype(BF)
    lo = (x - hi.astype(F32)).astype(BF)
    return hi, lo

def make(span, un):
    def kernel(bias, q_ref, g_ref, k_ref, v_ref, ctx_ref, dq_ref, dk_ref, dv_ref, k2, v2, s_ref, ph, plo):
        rows = k_ref.shape[0]
        nb = rows // span
        tiles = span // 128
        low = lax.broadcasted_iota(jnp.int32, (span, 128), 1) < 64
        q, near = q_ref[...], lax.broadcasted_iota(jnp.int32, (256, 128), 1) < 64
        q_hi = q.astype(BF).astype(F32)
        q_lo = q - q_hi
        qt = (q * LOG2E).T
        contexts, slopes = [], []
        gt = g_ref[...].T
        for head in range(2):
            def prepare(i, c):
                at = pl.ds(pl.multiple_of(i * span, span), span)
                for src, dst in ((k_ref, k2), (v_ref, v2)):
                    x = src[at, :]
                    hi = x.astype(BF).astype(F32)
                    lo = x - hi
                    if head == 0:
                        both = jnp.where(low, hi, pltpu.roll(lo, 64, 1))
                    else:
                        both = jnp.where(low, pltpu.roll(hi, 64, 1), lo)
                    dst[at, :] = both.astype(BF)
                return c
            lax.fori_loop(0, nb, prepare, 0)
            top = qt[head * 64:(head + 1) * 64]
            top_hi = top.astype(BF).astype(F32)
            top_lo = top - top_hi
            q4 = jnp.concatenate([top_hi, top_hi, top_lo, top_lo], axis=0).astype(BF)
            if head == 0:
                qn = jnp.where(near, q_hi, pltpu.roll(q_lo, 64, 1)).astype(BF)
            else:
                qn = jnp.where(near, pltpu.roll(q_hi, 64, 1), q_lo).astype(BF)

            def score(i, peak):
                at = pl.ds(pl.multiple_of(i * span, span), span)
                k = k2[at, :]
                s = dot_nn(jnp.concatenate([k, k], axis=1), q4)
                parts = []
                for t in range(tiles):
                    st = s[t * 128:(t + 1) * 128] + bias[pl.ds(i * tiles + t, 1), :]
                    s_ref[pl.ds(pl.multiple_of(i * span + t * 128, 128), 128), :] = st
                    peak = jnp.maximum(peak, jnp.max(st.reshape(16, 8, 256), axis=0))
                return peak
            peak = lax.fori_loop(0, nb, score, jnp.full((8, 256), -3e38, F32), unroll=un)
            peak = jnp.max(peak, axis=0, keepdims=True)

            def weigh(i, carry):
                total, acc = carry
                at = pl.ds(pl.multiple_of(i * span, span), span)
                p = jnp.exp2(s_ref[at, :] - peak)
                total = total + jnp.sum(p.reshape(span // 8, 8, 256), axis=0)
                hi, lo = halves(p)
                ph[at, :] = hi
                plo[at, :] = lo
                v = v2[at, :]
                acc = acc + dot_tn(v, hi) + dot_tn(v, lo)
                return total, acc
            total, acc = lax.fori_loop(0, nb, weigh, (jnp.zeros((8, 256), F32), jnp.zeros((128, 256), F32)), unroll=un)
            share = 1.0 / jnp.sum(total, axis=0, keepdims=True)
            ctx = (acc[:64] + acc[64:]) * share
            contexts.append(ctx)
            g = gt[head * 64:(head + 1) * 64] * share
            delta = jnp.sum(g * ctx, axis=0, keepdims=True)
            ghi = g.astype(BF).astype(F32)
            glo = g - ghi
            g2 = jnp.concatenate([ghi, glo], axis=0)
            g4 = jnp.concatenate([ghi, ghi, glo, glo], axis=0).astype(BF)
            gn = g2.T.astype(BF)

            def back(i, acc):
                at = pl.ds(pl.multiple_of(i * span, span), span)
                v = v2[at, :]
                k = k2[at, :]
                dp = dot_nn(jnp.concatenate([v, v], axis=1), g4)
                hi = ph[at, :]
                lo = plo[at, :]
                ds = (hi.astype(F32) + lo.astype(F32)) * (dp - delta)
                dv = dot_nn(hi, gn) + dot_nn(lo, gn)
                dv = dv + pltpu.roll(dv, 64, 1)
                shi, slo = halves(ds)
                dk = dot_nn(shi, qn) + dot_nn(slo, qn)
                dk = dk + pltpu.roll(dk, 64, 1)
                if head == 0:
                    dv_ref[at, :] = dv
                    dk_ref[at, :] = dk
                else:
                    dv_ref[at, :] = jnp.where(low, dv_ref[at, :], dv)
                    dk_ref[at, :] = jnp.where(low, dk_ref[at, :], dk)
                return acc + dot_tn(k, shi) + dot_tn(k, slo)
            acc = lax.fori_loop(0, nb, back, jnp.zeros((128, 256), F32), unroll=un)
            slopes.append(acc[:64] + acc[64:])
        ctx_ref[...] = jnp.concatenate(contexts, axis=0).T
        dq_ref[...] = jnp.concatenate(slopes, axis=0).T * 0.125

    def call(bias, q, g, kv):
        rows = kv.shape[0]
        pairs = 4
        return pl.pallas_call(
            kernel,
            grid=(pairs,),
            in_specs=[
                pl.BlockSpec(bias.shape, lambda p: (0, 0)),
                pl.BlockSpec((256, 128), lambda p: (0, p)),
                pl.BlockSpec((256, 128), lambda p: (0, p)),
                pl.BlockSpec((rows, 128), lambda p: (0, p)),
                pl.BlockSpec((rows, 128), lambda p: (0, 4 + p)),
            ],
            out_specs=[
                pl.BlockSpec((256, 128), lambda p: (0, p)),
                pl.BlockSpec((256, 128), lambda p: (0, p)),
                pl.BlockSpec((rows, 128), lambda p: (0, p)),
                pl.BlockSpec((rows, 128), lambda p: (0, p)),
            ],
            out_shape=[
                jax.ShapeDtypeStruct((256, 512), F32),
                jax.ShapeDtypeStruct((256, 512), F32),
                jax.ShapeDtypeStruct((rows, 512), F32),
                jax.ShapeDtypeStruct((rows, 512), F32),
            ],
            scratch_shapes=[
                pltpu.VMEM((rows, 128), BF),
                pltpu.VMEM((rows, 128), BF),
                pltpu.VMEM((rows, 256), F32),
                pltpu.VMEM((rows, 256), BF),
                pltpu.VMEM((rows, 256), BF),
            ],
            compiler_params=pltpu.CompilerParams(vmem_limit_bytes=56 * MIB),
            cost_estimate=pl.CostEstimate(flops=90_000_000_000, bytes_accessed=32 * MIB, transcendentals=8 * MIB),
        )(bias, q, g, kv, kv)
    return call

def tile_bias(tiles):
    return jnp.repeat(jnp.where(tiles.T > 0, 0.0, NEGATIVE).astype(F32), TILE, axis=1)


def front(pieces, slots, w_key, w_value, rows, span=512):
    width, n = 512, len(pieces)
    steps = rows // span
    part = 32
    count = sum(p.shape[0] for p in pieces)

    def kernel(idx, *refs):
        parts = refs[:n]
        wk, wv, x_ref, kv_ref, table, flat, wh, wl, sem = refs[n:]
        step = pl.program_id(0)

        @pl.when(step == 0)
        def _():
            copies, at = [], 0
            for j, p in enumerate(parts):
                copies.append(pltpu.make_async_copy(p, table.at[pl.ds(at, p.shape[0])], sem.at[j]))
                at += p.shape[0]
            for c in copies:
                c.start()
            for j, w in enumerate((wk, wv)):
                hi, lo = halves(w[...])
                wh[:, j * width:(j + 1) * width] = hi
                wl[:, j * width:(j + 1) * width] = lo
            for c in copies:
                c.wait()

        base = step * span

        def body(j, c):
            for u in range(part):
                e = j * part + u
                a = pl.multiple_of(idx[base + e], 4)
                b = pl.multiple_of(idx[rows + base + e], 4)
                flat[pl.ds(pl.multiple_of(e * 4, 4), 4), :] = table[pl.ds(a, 4), :] + table[pl.ds(b, 4), :]
            return c

        lax.fori_loop(0, span // part, body, 0)
        x = jnp.concatenate([flat[pl.ds(j, span, stride=4), :] for j in range(4)], axis=1)
        x_ref[...] = x
        hi, lo = halves(x)
        kv_ref[...] = dot_nn(hi, wh[...]) + dot_nn(hi, wl[...]) + dot_nn(lo, wh[...])

    whole = pl.BlockSpec((width, width), lambda i: (0, 0))
    return pl.pallas_call(
        kernel,
        grid=(steps,),
        in_specs=[pl.BlockSpec(memory_space=pltpu.SMEM)] + [pl.BlockSpec(memory_space=pl.ANY)] * n + [whole] * 2,
        out_specs=[
            pl.BlockSpec((span, width), lambda i: (i, 0)),
            pl.BlockSpec((span, 2 * width), lambda i: (i, 0)),
        ],
        out_shape=[jax.ShapeDtypeStruct((rows, width), F32), jax.ShapeDtypeStruct((rows, 2 * width), F32)],
        scratch_shapes=[
            pltpu.VMEM((count, 128), F32),
            pltpu.VMEM((span * 4, 128), F32),
            pltpu.VMEM((width, 2 * width), BF),
            pltpu.VMEM((width, 2 * width), BF),
            pltpu.SemaphoreType.DMA((n,)),
        ],
        compiler_params=pltpu.CompilerParams(vmem_limit_bytes=56 * MIB),
        cost_estimate=pl.CostEstimate(flops=40_000_000_000, bytes_accessed=32 * MIB, transcendentals=0),
    )(slots, *pieces, w_key, w_value)


def back(slots, own, dk, dv, w_key, w_value, qx, count, span=512):
    rows, width = dk.shape
    steps = rows // span
    part = 32
    quarter = count

    def kernel(idx, own_ref, dk_ref, dv_ref, wk, wv, qx_ref, *refs):
        outs, accs = refs[:4], refs[4:8]
        dx, flat, wh, wl, sem = refs[8:]
        step = pl.program_id(0)

        @pl.when(step == 0)
        def _():
            def clear(i, c):
                at = pl.ds(pl.multiple_of(i * 512, 512), 512)
                for a in accs:
                    a[at, :] = jnp.zeros((512, 128), F32)
                return c

            lax.fori_loop(0, count * 4 // 512, clear, 0)
            for j, w in enumerate((wk, wv)):
                hi, lo = halves(w[...].T)
                wh[j * width:(j + 1) * width, :] = hi
                wl[j * width:(j + 1) * width, :] = lo

        khi, klo = halves(dk_ref[...])
        vhi, vlo = halves(dv_ref[...])
        hi = jnp.concatenate([khi, vhi], axis=1)
        lo = jnp.concatenate([klo, vlo], axis=1)
        dx[...] = dot_nn(hi, wh[...]) + dot_nn(hi, wl[...]) + dot_nn(lo, wh[...])

        @pl.when(own_ref[0] // 2 == step)
        def _():
            at = pl.ds(pl.multiple_of(own_ref[0] % 2 * 256, 256), 256)
            dx[at, :] += qx_ref[...]

        for j in range(4):
            flat[pl.ds(j, span, stride=4), :] = dx[:, j * 128:(j + 1) * 128]
        base = step * span

        def body(j, c):
            for u in range(part):
                e = j * part + u
                a = pl.multiple_of(idx[base + e], 4)
                b = pl.multiple_of(idx[rows + base + e], 4)
                row = flat[pl.ds(pl.multiple_of(e * 4, 4), 4), :]
                k = u % 2 * 2
                accs[k][pl.ds(a, 4), :] += row
                accs[k + 1][pl.ds(b, 4), :] += row
            return c

        lax.fori_loop(0, span // part, body, 0)

        @pl.when(step == steps - 1)
        def _():
            copies = []
            for q in range(4):
                def add(i, c):
                    at = pl.ds(pl.multiple_of(q * quarter + i * 512, 512), 512)
                    accs[0][at, :] = (accs[0][at, :] + accs[1][at, :]) + (accs[2][at, :] + accs[3][at, :])
                    return c

                lax.fori_loop(0, quarter // 512, add, 0)
                copies.append(pltpu.make_async_copy(accs[0].at[pl.ds(q * quarter, quarter)], outs[q], sem.at[q]))
                copies[-1].start()
            for c in copies:
                c.wait()

    whole = pl.BlockSpec((width, width), lambda i: (0, 0))
    return pl.pallas_call(
        kernel,
        grid=(steps,),
        in_specs=[pl.BlockSpec(memory_space=pltpu.SMEM)] * 2
        + [pl.BlockSpec((span, width), lambda i: (i, 0))] * 2
        + [whole] * 2
        + [pl.BlockSpec(qx.shape, lambda i: (0, 0))],
        out_specs=[pl.BlockSpec(memory_space=pl.ANY)] * 4,
        out_shape=[jax.ShapeDtypeStruct((quarter, 128), F32)] * 4,
        scratch_shapes=[pltpu.VMEM((count * 4, 128), F32)] * 4
        + [
            pltpu.VMEM((span, width), F32),
            pltpu.VMEM((span * 4, 128), F32),
            pltpu.VMEM((2 * width, width), BF),
            pltpu.VMEM((2 * width, width), BF),
            pltpu.SemaphoreType.DMA((4,)),
        ],
        compiler_params=pltpu.CompilerParams(vmem_limit_bytes=58 * MIB),
        cost_estimate=pl.CostEstimate(flops=40_000_000_000, bytes_accessed=24 * MIB, transcendentals=0),
    )(slots, own, dk, dv, w_key, w_value, qx)


def weight_blocks(places, dq_w, do_w, dk, dv, x, span=512):
    rows, width = x.shape
    steps = rows // span

    def kernel(at_ref, q_ref, o_ref, dk_ref, dv_ref, x_ref, *refs):
        outs, out_ref, w_ref, sem = refs[:4], *refs[4:]
        @pl.when(pl.program_id(0) == 0)
        def _():
            w_ref[...] = jnp.zeros_like(w_ref)

        xhi, xlo = halves(x_ref[...])
        for j, ref in enumerate((dk_ref, dv_ref)):
            hi, lo = halves(ref[...])
            w_ref[:, j * width:(j + 1) * width] += dot_tn(xhi, hi) + dot_tn(xhi, lo) + dot_tn(xlo, hi)

        @pl.when(pl.program_id(0) == steps - 1)
        def _():
            def copy(i, c):
                cut = pl.ds(pl.multiple_of(i * 16, 16), 16)
                for j in range(16):
                    ref, k = ((w_ref, j), (q_ref, j - 8), (o_ref, j - 12))[(j >= 8) + (j >= 12)]
                    to = pl.ds(pl.multiple_of(at_ref[i * 16 + j] * 16, 16), 16)
                    out_ref[to, :] = ref[cut, k * 128:(k + 1) * 128]
                return c

            lax.fori_loop(0, 32, copy, 0)
            copies = [pltpu.make_async_copy(out_ref.at[pl.ds(j * 4 * width, 4 * width)], outs[j], sem.at[j]) for j in range(4)]
            for c in copies:
                c.start()
            for c in copies:
                c.wait()

    whole = pl.BlockSpec((width, width), lambda i: (0, 0))
    return pl.pallas_call(
        kernel,
        grid=(steps,),
        in_specs=[pl.BlockSpec(memory_space=pltpu.SMEM), whole, whole]
        + [pl.BlockSpec((span, width), lambda i: (i, 0))] * 3,
        out_specs=[pl.BlockSpec(memory_space=pl.ANY)] * 4,
        out_shape=[jax.ShapeDtypeStruct((4 * width, 128), F32)] * 4,
        scratch_shapes=[
            pltpu.VMEM((16 * width, 128), F32),
            pltpu.VMEM((width, 2 * width), F32),
            pltpu.SemaphoreType.DMA((4,)),
        ],
        compiler_params=pltpu.CompilerParams(vmem_limit_bytes=56 * MIB),
        cost_estimate=pl.CostEstimate(flops=20_000_000_000, bytes_accessed=28 * MIB, transcendentals=0),
    )(places, dq_w, do_w, dk, dv, x)


def weights_of(places, pieces):
    width = 512
    n = len(pieces)

    def kernel(at_ref, *refs):
        parts, outs, all_ref, sem = refs[:n], refs[n:n + 4], refs[n + 4], refs[n + 5]
        copies, base = [], 0
        for j, p in enumerate(parts):
            copies.append(pltpu.make_async_copy(p, all_ref.at[pl.ds(base, p.shape[0])], sem.at[j]))
            base += p.shape[0]
        for c in copies:
            c.start()
        for c in copies:
            c.wait()

        def copy(i, c):
            cut = pl.ds(pl.multiple_of(i * 16, 16), 16)
            for j in range(16):
                k = j % 4
                at = pl.ds(pl.multiple_of(at_ref[i * 16 + j] * 16, 16), 16)
                outs[j // 4][cut, k * 128:(k + 1) * 128] = all_ref[at, :]
            return c

        lax.fori_loop(0, 32, copy, 0)

    return pl.pallas_call(
        kernel,
        in_specs=[pl.BlockSpec(memory_space=pltpu.SMEM)] + [pl.BlockSpec(memory_space=pl.ANY)] * n,
        out_specs=[pl.BlockSpec(memory_space=pltpu.VMEM)] * 4,
        out_shape=[jax.ShapeDtypeStruct((width, width), F32)] * 4,
        scratch_shapes=[pltpu.VMEM((16 * width, 128), F32), pltpu.SemaphoreType.DMA((n,))],
        compiler_params=pltpu.CompilerParams(vmem_limit_bytes=56 * MIB),
    )(places, *pieces)


Z = ("zl", "zh")
SIZES = {"x": 4, "y": 4, Z: 4, "c": 2}


def place(axis, i):
    return i % 2 * 2 + i // 2 if axis == Z else i


def move(v, axis, to):
    n = SIZES[axis]
    return lax.ppermute(v, axis, [(place(axis, i), place(axis, to(i))) for i in range(n)])


def shift(v, axis, s):
    return move(v, axis, lambda i: (i + s) % SIZES[axis])


def further(v, before, after, axis):
    n = v.shape[0] // 2
    return [v, before, after, shift(before[:n], axis, 1), shift(after[n:], axis, -1)]


def table_gather(shard, lists, rows_of, places_of, extra):
    c = lax.axis_index("c")
    half = shard.shape[0] // 2
    mine = lax.dynamic_slice_in_dim(shard, c * half, half, 0)
    a1, a2 = mine[:half // 2], mine[half // 2:]
    before, after = shift(a1, "x", 1), shift(a1, "x", -1)
    q = half // 4
    za, zb = shift(a2[:q], Z, 1), shift(a2[q:], Z, -1)
    v2 = jnp.concatenate([a2, za, zb], 0)
    v2, before, after, lists = lax.optimization_barrier((v2, before, after, lists))
    s1 = further(a1, before, after, "x")
    before2, after2 = shift(v2, "x", 1), shift(v2, "x", -1)
    rows = rows_of(lists)
    up, down = jnp.concatenate(s1[:2], 0), jnp.concatenate(s1[2:], 0)
    z1, z2 = shift(up, Z, 1), shift(down, Z, -1)
    before2, after2, rows = lax.optimization_barrier((before2, after2, rows))
    s2 = further(v2, before2, after2, "x")
    s2[-1], places, extra = lax.optimization_barrier((s2[-1], places_of(rows), extra))
    own = [up, down, z1, z2] + s2
    return own + [shift(v, "c", 1) for v in own], places, extra


SIDES = (lambda i: i ^ 1, lambda i: 3 - i)
GROUPS = (
    ((("x", 0), ("x", 1)), (("y", 0), ("y", 1), (Z, 0), (Z, 1))),
    ((("y", 0), ("y", 1)), ((Z, 0), (Z, 1), ("x", 0), ("x", 1))),
)


def side_bit(bit, at):
    axis, side = bit
    return (at[axis] + 1) // 2 % 2 if side == 0 else at[axis] // 2


def across(v, bit):
    return move(v, bit[0], SIDES[bit[1]])


def halve(v, dim, bit):
    keep = lax.index_in_dim(v, 0, dim, keepdims=False)
    send = lax.index_in_dim(v, 1, dim, keepdims=False)
    return keep + across(send, bit)


def sum_over_devices(terms, blocks, extra):
    bits = [2] * 6
    terms = [v.reshape(2, *bits, -1, 128) for v in terms]
    blocks = [v.reshape(2, *bits, -1, 128) for v in blocks]
    n = terms[0].shape[-2]
    mine, pieces = [], []
    for g, (first, rest) in enumerate(GROUPS):
        sent = shift(jnp.concatenate([terms[2 * g + 1], blocks[2 * g + 1]], axis=-2), "c", 1)
        v = jnp.concatenate([terms[2 * g], blocks[2 * g]], axis=-2) + sent
        a = halve(halve(v[0], 0, first[0]), 0, first[1])
        b = halve(v[1], 0, first[1])
        if g == 0:
            b, extra = lax.optimization_barrier((b, extra))
        b = halve(b, 0, first[0])
        w = jnp.stack([a, b])
        for bit in rest:
            w = halve(w, 1, bit)
        mine.append(w[:, :n])
        w = w[:, n:]
        for bit in rest[::-1]:
            w = jnp.stack([w, across(w, bit)], axis=1)
        a, b = w[0], w[1]
        for bit in first[::-1]:
            a = jnp.stack([a, across(a, bit)])
        for bit in first:
            b = jnp.stack([b, across(b, bit)])
        w = jnp.stack([a, b]).reshape(-1, 128)
        pieces += [w, shift(w, "c", 1)]
    return jnp.stack(mine).reshape(-1, 128), pieces, extra


def coordinates():
    zl, x, y, zh, c = (lax.axis_index(a) for a in ("zl", "x", "y", "zh", "c"))
    return {"x": x, "y": y, Z: zh * 2 + zl, "c": c, "zl": zl, "zh": zh}


def table_place(row, me):
    owner, local = row // 512, row % 512
    half, part, within = local // 256, local % 256 // 128, local % 128
    turn = (owner % 4 - me["x"]) % 4
    order = jnp.where(turn == 0, 0, jnp.where(turn == 3, 1, jnp.where(turn == 1, 2, 3)))
    other = (owner // 4 != me["zl"]).astype(jnp.int32)
    first = other * 512 + order * 128 + within
    second = 1024 + order * 256 + other * 128 + within
    return jnp.where(half != me["c"], 2048, 0) + jnp.where(part == 0, first, second)


def scatter_place(row, me):
    owner, local = row // 512, row % 512
    seq, within = local // 32, local % 32
    at = {"x": owner % 4, "y": seq // 4, Z: seq // 2 % 2 * 2 + owner // 4, "c": seq % 2}
    group, sub, inner = within // 16, within // 8 % 2, within % 8

    def chain(bits):
        out = 0
        for bit in bits:
            out = out * 2 + (side_bit(bit, at) ^ side_bit(bit, me))
        return out

    spots = []
    for first, rest in GROUPS:
        lead = jnp.where(sub == 0, chain(first), chain(first[::-1]))
        spots.append(lead * 16 + chain(rest))
    spot = jnp.where(group == 0, *spots)
    return (((group * 2 + (at["c"] ^ me["c"])) * 2 + sub) * 64 + spot) * 8 + inner


def block_place(me):
    ids = jnp.arange(512, dtype=jnp.int32)
    group, sub = ids // 256, ids // 64 % 2

    def chain(bits):
        out = 0
        for bit in bits:
            out = out * 2 + side_bit(bit, me)
        return out

    spots = []
    for first, rest in GROUPS:
        lead = jnp.where(sub == 0, chain(first), chain(first[::-1]))
        spots.append(lead * 16 + chain(rest))
    return ids ^ (jnp.where(group == 0, *spots) + me["c"] * 128)


DP = ("zl", "x")
SEQ = ("y", "zh", "c")


def on_device(
    item_table,
    serve_lists,
    event_slots,
    session_tiles,
    w_query,
    w_key,
    w_value,
    w_out,
    grad_attended,
):
    me = coordinates()
    seq = lax.axis_index(SEQ)
    slots = event_slots[0]

    def rows_of(lists):
        rows = slots // TILE * 512 + lists.reshape(-1)[slots]
        rows = jnp.broadcast_to(rows.reshape(1, 4, 128), (16, 4, 128))
        return lax.all_to_all(rows, SEQ, split_axis=0, concat_axis=0, tiled=True)

    def places_of(rows):
        rows = rows.reshape(16, 2, 256).transpose(1, 0, 2).reshape(2, 4096)
        return [(place(rows, me) * 4).reshape(-1) for place in (table_place, scatter_place)]

    cotangent = grad_attended[0]
    lists = lax.all_to_all(serve_lists[0, :, 0, :], DP, split_axis=0, concat_axis=0, tiled=True)
    pieces, (from_places, to_places), (grad_context, bias) = table_gather(
        item_table.reshape(-1, 128),
        lists,
        rows_of,
        places_of,
        (product(cotangent, w_out.T), tile_bias(session_tiles[0])),
    )
    history, both = front(pieces, from_places, w_key, w_value, 4096)
    inputs = lax.dynamic_slice_in_dim(history, seq * 256, 256, 0)
    scale = HEAD_DIM ** (-0.5)
    queries = product(inputs, w_query, EXACT) * scale
    context, grad_queries, grad_keys, grad_values = make(SPAN, 2)(
        bias, queries, grad_context, both
    )
    attended = product(context, w_out)
    grad_out_w = product(context.T, cotangent)
    grad_query_w = product(inputs.T, grad_queries)
    query_terms = product(grad_queries, w_query.T)
    places = block_place(me)
    blocks = weight_blocks(places, grad_query_w, grad_out_w, grad_keys, grad_values, history)
    terms = back(
        to_places, seq.reshape(1), grad_keys, grad_values, w_key, w_value, query_terms, 4096
    )
    grad_table, pieces, attended = sum_over_devices(terms, blocks, attended)
    grad_key_w, grad_value_w, grad_query_w, grad_out_w = weights_of(places, pieces)
    grad_table = grad_table.reshape(32, 512)
    return (attended[None], grad_query_w, grad_key_w, grad_value_w, grad_out_w, grad_table)


def solution(mesh):
    fine = Mesh(mesh.devices.reshape(2, 4, 4, 2, 2), ("zl", "x", "y", "zh", "c"))
    return jax.shard_map(
        on_device,
        mesh=fine,
        in_specs=(
            P(DP, None),
            P(DP, None, SEQ, None),
            P(DP, None, SEQ),
            P(DP, SEQ, None),
            P(),
            P(),
            P(),
            P(),
            P(DP, SEQ, None),
        ),
        out_specs=(P(DP, SEQ, None), P(), P(), P(), P(), P(DP + SEQ, None)),
        check_vma=False,
    )
```
